32 devices in a mesh: dp: 8 (over y, x, core), tensor: 4 (over z).
Axes of the slice: x: 2, y: 2, z: 4, core: 2. Of those that a mesh axis runs over, the one named last changes fastest.
Arguments:
- hidden: bfloat16 [8, 2048, 1024], P('dp', 'tensor'), may hold values from -6 to 6
- segment_ids: int32 [8, 2048], P('dp'), may hold values from 0 to 3, never falling along the last dimension, each value on 1 to 1024 neighbouring positions
- norm_gain: float32 [1024], replicated, may hold values from 0.5 to 1.5
- w_z: bfloat16 [1024, 2048], P(None, 'tensor'), may hold values from -0.1875 to 0.1875
- w_x: bfloat16 [1024, 2048], P(None, 'tensor'), may hold values from -0.1875 to 0.1875
- w_bc: bfloat16 [1024, 256], replicated, may hold values from -0.1875 to 0.1875
- w_dt: bfloat16 [1024, 32], P(None, 'tensor'), may hold values from -0.1875 to 0.1875
- conv_x_w: float32 [4, 2048], P(None, 'tensor'), may hold values from -3 to 3
- conv_x_b: float32 [2048], P('tensor'), may hold values from -2 to 2
- conv_bc_w: float32 [4, 256], replicated, may hold values from -3 to 3
- conv_bc_b: float32 [256], replicated, may hold values from -2 to 2
- dt_bias: float32 [32], P('tensor'), may hold values from -5 to -2
- a_log: float32 [32], P('tensor'), may hold values from -1 to 2.8
- skip_d: float32 [32], P('tensor'), may hold values from 0.5 to 2
- gate_gain: float32 [2048], P('tensor'), may hold values from 0.5 to 1.5
- w_out: bfloat16 [2048, 1024], P('tensor'), may hold values from -0.125 to 0.125
- cotangent: bfloat16 [8, 2048, 1024], P('dp', 'tensor'), may hold values from -6 to 6
Outputs:
- block_out: bfloat16 [8, 2048, 1024], P('dp', 'tensor')
- grad_hidden: float32 [8, 2048, 1024], P('dp', 'tensor')
- grad_norm_gain: float32 [1024], replicated
- grad_w_z: float32 [1024, 2048], P(None, 'tensor')
- grad_w_x: float32 [1024, 2048], P(None, 'tensor')
- grad_w_bc: float32 [1024, 256], replicated
- grad_w_dt: float32 [1024, 32], P(None, 'tensor')
- grad_conv_x_w: float32 [4, 2048], P(None, 'tensor')
- grad_conv_x_b: float32 [2048], P('tensor')
- grad_conv_bc_w: float32 [4, 256], replicated
- grad_conv_bc_b: float32 [256], replicated
- grad_dt_bias: float32 [32], P('tensor')
- grad_a_log: float32 [32], P('tensor')
- grad_skip_d: float32 [32], P('tensor')
- grad_gate_gain: float32 [2048], P('tensor')
- grad_w_out: float32 [2048, 1024], P('tensor')
The draws below stay inside these ranges and needn't reach their ends.
Inputs may be any that keep to these rules, and one draw needn't show every extreme that they name: `segment_ids`: along each sequence the document numbers never fall; a document holds 1 to 1024 tokens, and in every sequence one holds exactly 1024.
All inputs are finite; a program needn't handle non-finite values.
Results may differ from the reference program's by a relative error of at most 0.0083.
Values may be sent and summed in bfloat16 or wider, within the bound.
No kernel may reach another device: no remote copies, remote signals or barrier semaphores. Data moves between devices by JAX's collectives and lax.ppermute only.
A program may use at most 128 MiB of HBM per device.

```python
import math
import jax
import jax.numpy as jnp
import numpy as np
from jax import lax

D = 1024
H = 32
N = 128
K = 4
CH = 256
SEGS = 4
L = 2048
DI = 2048
NSEQ = 8


def block_scale(rng, extent, split, least, largest):
    gain = 1.0
    for position, parts in split:
        heights = jax.random.uniform(jax.random.fold_in(jax.random.fold_in(rng, 6), position), (parts,), jnp.float32, least / len(split), largest / len(split))
        gain = gain * jnp.repeat(jnp.exp(heights), extent[position] // parts).reshape((-1,) + (1,) * (len(extent) - 1 - position))
    return gain


def length_profile(count, total, limit, skew):
    portions = [(1 << 20) // math.isqrt(standing ** skew) + 1 for standing in range(2, count + 1)]
    surplus, holding = total - limit - (count - 1), [1] * (count - 1)
    while surplus > 0:
        candidates = [i for i in range(count - 1) if holding[i] < limit]
        whole, budget = sum([portions[i] for i in candidates]), surplus
        for i in candidates:
            addition = min(limit - holding[i], max(1, budget * portions[i] // whole), surplus)
            holding[i] = holding[i] + addition
            surplus = surplus - addition
    return np.array([limit] + holding)


def uneven_parts(key, number_of, total, bound, slope):
    if number_of == 2:
        one = jax.random.randint(key, (), max(1, total - bound), min(bound, total - 1) + 1)
        return jnp.stack([one, total - one])
    tallies = jnp.asarray(length_profile(number_of, total, bound, slope), jnp.int32)
    pairs = (number_of - 1) // 2
    source_of, receiver = tallies[1:1 + 2 * pairs:2], tallies[2:2 + 2 * pairs:2]
    room = jnp.minimum(source_of - 1, bound - receiver)
    moved = jax.random.randint(jax.random.fold_in(key, 1), (pairs,), 0, 1 << 20) % (room + 1)
    tallies = tallies.at[1:1 + 2 * pairs:2].set(source_of - moved).at[2:2 + 2 * pairs:2].set(receiver + moved)
    return tallies[jax.random.permutation(jax.random.fold_in(key, 2), number_of)]


def scatter_about(key, dims, spread, limit, shards=(), held_as=jnp.bfloat16):
    loudness = block_scale(key, dims, shards, -0.22, 0.18) if shards else 1.0
    drawn = jax.random.normal(key, dims, jnp.float32) * spread * loudness
    return jnp.minimum(jnp.maximum(drawn, -limit), limit).astype(held_as)


def setup_inputs(seed: int = 0) -> dict:
    seeds = jax.random.split(jax.random.key(seed), 18)
    hidden = scatter_about(seeds[0], (NSEQ, L, D), 1.0, 6.0, ((0, 8), (1, 4)))
    segment_ids = jax.vmap(lambda own: jnp.searchsorted(jnp.cumsum(uneven_parts(own, SEGS, L, L // 2, 1)), jnp.arange(L), side="right"))(jax.random.split(seeds[1], NSEQ)).reshape((NSEQ, L)).astype(jnp.int32)
    norm_gain = jnp.clip(1.0 + 0.1 * jax.random.normal(seeds[2], (D,), jnp.float32), 0.5, 1.5)
    w_z = scatter_about(seeds[3], (D, DI), D ** -0.5, 0.1875, ((1, 4),))
    w_x = scatter_about(seeds[4], (D, DI), D ** -0.5, 0.1875, ((1, 4),))
    w_bc = scatter_about(seeds[5], (D, 2 * N), D ** -0.5, 0.1875)
    w_dt = scatter_about(seeds[6], (D, H), D ** -0.5, 0.1875, ((1, 4),))
    conv_x_w = scatter_about(seeds[7], (K, DI), K ** -0.5, 3.0, ((1, 4),), jnp.float32)
    conv_x_b = scatter_about(seeds[8], (DI,), 0.3, 2.0, ((0, 4),), jnp.float32)
    conv_bc_w = scatter_about(seeds[9], (K, 2 * N), K ** -0.5, 3.0, (), jnp.float32)
    conv_bc_b = scatter_about(seeds[10], (2 * N,), 0.3, 2.0, (), jnp.float32)
    dt_bias = jnp.clip(-5.0 + 3.0 * jax.random.uniform(seeds[11], (H,), jnp.float32) ** block_scale(seeds[11], (H,), ((0, 4),), -0.2, 0.2), -5.0, -2.0)
    a_log = jnp.clip(-1.0 + 3.8 * jax.random.uniform(seeds[12], (H,), jnp.float32) ** block_scale(seeds[12], (H,), ((0, 4),), -0.2, 0.2), -1.0, 2.8)
    skip_d = jnp.clip(0.5 + 1.5 * jax.random.uniform(seeds[13], (H,), jnp.float32) ** block_scale(seeds[13], (H,), ((0, 4),), -0.2, 0.2), 0.5, 2.0)
    gate_gain = jnp.clip(1.0 + 0.1 * jax.random.normal(seeds[14], (DI,), jnp.float32), 0.5, 1.5)
    w_out = scatter_about(seeds[15], (DI, D), DI ** -0.5, 0.125, ((0, 4),))
    cotangent = scatter_about(seeds[16], (NSEQ, L, D), 1.0, 6.0, ((0, 8), (1, 4)))
    return dict(hidden=hidden, segment_ids=segment_ids, norm_gain=norm_gain, w_z=w_z, w_x=w_x, w_bc=w_bc, w_dt=w_dt, conv_x_w=conv_x_w, conv_x_b=conv_x_b, conv_bc_w=conv_bc_w, conv_bc_b=conv_bc_b, dt_bias=dt_bias, a_log=a_log, skip_d=skip_d, gate_gain=gate_gain, w_out=w_out, cotangent=cotangent)


@jax.custom_vjp
def low(v):
    return lax.optimization_barrier(v.astype(jnp.bfloat16)).astype(jnp.float32)

@jax.custom_vjp
def low_back(v):
    return v

def low_keep(v):
    return (low(v), None)

def low_pass(kept, grad):
    return (grad,)

def back_keep(v):
    return (v, None)

def back_low(kept, grad):
    return (low(grad),)
low.defvjp(low_keep, low_pass)
low_back.defvjp(back_keep, back_low)
epsilon = 1e-05
highest = lax.Precision.HIGHEST

def matmul_hi(left, right):
    return jnp.dot(left, right, precision=highest, preferred_element_type=jnp.float32)

def shifted(values, doc_ids, offset):
    if offset == 0:
        return values
    zero_rows = jnp.zeros((offset, values.shape[1]), values.dtype)
    moved_rows = jnp.concatenate([zero_rows, values[:-offset]], 0)
    doc_moved = jnp.concatenate([jnp.full((offset,), -1, jnp.int32), doc_ids[:-offset].astype(jnp.int32)], 0)
    return jnp.where((doc_moved == doc_ids.astype(jnp.int32))[:, None], moved_rows, 0.0)

def causal_conv(values, weight, bias_row, doc_ids):
    tap_count = weight.shape[0]
    result = bias_row[None, :] + weight[tap_count - 1][None, :] * values
    for offset in range(1, tap_count):
        result = result + weight[tap_count - 1 - offset][None, :] * shifted(values, doc_ids, offset)
    return result

def ssd_heads(xs, states, dt_raw, dt_bias, a_log, skip_d, doc_ids):
    seq_len, inner_dim = xs.shape
    head_count = dt_raw.shape[1]
    head_dim = inner_dim // head_count
    state_dim = states.shape[1] // 2
    block_count = seq_len // CH
    step_size = jax.nn.softplus(dt_raw + dt_bias)
    log_decay = step_size * -jnp.exp(a_log)
    x_heads = xs.reshape(seq_len, head_count, head_dim)
    inputs = x_heads * step_size[:, :, None]
    blocked = (inputs.reshape(block_count, CH, head_count, head_dim), states[:, :state_dim].reshape(block_count, CH, state_dim), states[:, state_dim:].reshape(block_count, CH, state_dim), log_decay.reshape(block_count, CH, head_count), doc_ids.astype(jnp.int32).reshape(block_count, CH))
    positions = lax.broadcasted_iota(jnp.int32, (CH, CH), 0)
    columns = lax.broadcasted_iota(jnp.int32, (CH, CH), 1)

    def block_step(carried, seq_item):
        state_now, prev_doc = carried
        inputs_blk, b_block, c_block, decay_blk, doc_blk = seq_item
        cum_decay = jnp.cumsum(decay_blk, 0)
        gram_mat = jnp.dot(c_block, b_block.T, precision=highest, preferred_element_type=jnp.float32)
        same_doc = (doc_blk[:, None] == doc_blk[None, :]) & (positions >= columns)
        cum_heads = cum_decay.T
        exp_arg = jnp.where(same_doc[None], cum_heads[:, :, None] - cum_heads[:, None, :], 0.0)
        weight_mat = jnp.where(same_doc[None], jnp.exp(exp_arg), 0.0) * gram_mat[None]
        intra_out = jnp.einsum('hts,shp->thp', weight_mat, inputs_blk, precision=highest)
        carry_mask = (doc_blk == prev_doc).astype(jnp.float32)
        carried_out = jnp.einsum('tn,hnp->thp', c_block, state_now, precision=highest)
        carried_out = carried_out * (jnp.exp(cum_decay) * carry_mask[:, None])[:, :, None]
        last_doc = doc_blk[CH - 1].astype(jnp.int32)
        keep_mask = (doc_blk == last_doc).astype(jnp.float32)
        tail_decay = jnp.exp(cum_decay[CH - 1][None, :] - cum_decay) * keep_mask[:, None]
        fresh_state = jnp.einsum('sn,shp->hnp', b_block, inputs_blk * tail_decay[:, :, None], precision=highest)
        kept_share = jnp.exp(cum_decay[CH - 1]) * (last_doc == prev_doc).astype(jnp.float32)
        new_state = state_now * kept_share[:, None, None] + fresh_state
        return ((new_state, last_doc), intra_out + carried_out)
    init_carry = (jnp.zeros((head_count, state_dim, head_dim), jnp.float32), jnp.array(-1, jnp.int32))
    _, block_outs = lax.scan(block_step, init_carry, blocked)
    y_heads = block_outs.reshape(seq_len, head_count, head_dim) + skip_d[None, :, None] * x_heads
    return y_heads.reshape(seq_len, inner_dim)

def layer_forward(params, tok_rows, doc_ids):
    norm_gain, w_z, w_x, w_bc, w_dt, conv_x_w, conv_x_b, conv_bc_w, conv_bc_b, dt_bias, a_log, skip_d, gate_gain, w_out = params
    inv_norm = lax.rsqrt(lax.optimization_barrier(jnp.mean(tok_rows * tok_rows, -1, keepdims=True)) + epsilon)
    normed = low(tok_rows * inv_norm * norm_gain)
    z_raw = low_back(matmul_hi(normed, w_z))
    x_raw = low_back(matmul_hi(normed, w_x))
    bc_raw = matmul_hi(normed, w_bc)
    dt_raw = low_back(matmul_hi(normed, w_dt))
    xs = jax.nn.silu(causal_conv(x_raw, conv_x_w, conv_x_b, doc_ids))
    states = jax.nn.silu(causal_conv(bc_raw, conv_bc_w, conv_bc_b, doc_ids))
    y_out = ssd_heads(xs, states, dt_raw, dt_bias, a_log, skip_d, doc_ids)
    gated_out = y_out * jax.nn.silu(z_raw)
    inv_gate = lax.rsqrt(lax.optimization_barrier(jnp.mean(gated_out * gated_out, -1, keepdims=True)) + epsilon)
    normed_gate = low(gated_out * inv_gate * gate_gain)
    return tok_rows + matmul_hi(normed_gate, w_out)

def reference(hidden, segment_ids, norm_gain, w_z, w_x, w_bc, w_dt, conv_x_w, conv_x_b, conv_bc_w, conv_bc_b, dt_bias, a_log, skip_d, gate_gain, w_out, cotangent):
    params = tuple((item.astype(jnp.float32) for item in (norm_gain, w_z, w_x, w_bc, w_dt, conv_x_w, conv_x_b, conv_bc_w, conv_bc_b, dt_bias, a_log, skip_d, gate_gain, w_out)))
    seg_all = segment_ids.astype(jnp.int32)

    def per_sequence(totals, seq_item):
        tok_rows, doc_ids, cot_rows = seq_item

        def run_layer(weights, inputs):
            return layer_forward(weights, inputs, doc_ids)
        block_rows, pull_back = jax.vjp(run_layer, params, tok_rows.astype(jnp.float32))
        grad_params, grad_rows = pull_back(cot_rows.astype(jnp.float32))
        totals = jax.tree.map(jnp.add, totals, grad_params)
        return (totals, (block_rows.astype(jnp.bfloat16), grad_rows))
    zero_grads = tuple((jnp.zeros_like(item) for item in params))
    totals, (seq_outs, grad_seqs) = lax.scan(per_sequence, zero_grads, (hidden, seg_all, cotangent))
    return (seq_outs, grad_seqs, totals[0], totals[1], totals[2], totals[3], totals[4], totals[5], totals[6], totals[7], totals[8], totals[9], totals[10], totals[11], totals[12], totals[13])
```

```python
import jax
import jax.numpy as jnp
from jax import lax
from jax.experimental import pallas as pl
from jax.experimental.pallas import tpu as pltpu
from jax.sharding import PartitionSpec as P

CH = 256
HALO = 16
DOC_MAX = 1024
GROUP = 8
SLOT = 8
LANES = 128
TAIL_ROWS = 32
HEAD_DIM = 64
epsilon = 1e-05
F32 = jnp.float32
BF16 = jnp.bfloat16
CUM, STEP, FADE, TAIL, HEAD = range(5)
CONV_B, GAIN, SKIP, FLAT, W_DT = 4, 5, 6, 7, 8


def mm(a, b):
    return jnp.dot(a, b, preferred_element_type=F32)


def mm_nt(a, b):
    return lax.dot_general(a, b, (((1,), (1,)), ((), ())), preferred_element_type=F32)


def mm_tn(a, b):
    return lax.dot_general(a, b, (((0,), (0,)), ((), ())), preferred_element_type=F32)


def swap(x, axis, k):
    n = lax.axis_size(axis)
    return lax.ppermute(x, axis, [(i, i ^ k) for i in range(n)])


def shift_up(x, axis, by):
    n = lax.axis_size(axis)
    return lax.ppermute(x, axis, [(i, i + by) for i in range(n) if 0 <= i + by < n])


def gather_blocks(mine):
    zs = lax.axis_size("tensor")
    return jnp.stack([swap(mine, "tensor", k) for k in range(1, zs)], 0)


def spread_pieces(got):
    even = [got] + [swap(got, "dp", m) for m in (2, 4, 6)]
    pieces = []
    for part in even:
        pieces += [part, swap(part, "dp", 1)]
    return pieces


def total(parts):
    acc = parts[0].astype(F32)
    for part in parts[1:]:
        acc = acc + part.astype(F32)
    return acc


def call(body, grid, in_specs, out_specs, out_shapes, scratch, scalars, args, us=0.3, deps=()):
    n_in, n_deps = len(args), len(deps)

    def run(s, *refs):
        body(s, *refs[:n_in], *refs[n_in + n_deps :])

    return pl.pallas_call(
        run,
        grid_spec=pltpu.PrefetchScalarGridSpec(
            num_scalar_prefetch=1,
            grid=grid,
            in_specs=list(in_specs) + [pl.BlockSpec(memory_space=pl.ANY)] * n_deps,
            out_specs=out_specs,
            scratch_shapes=scratch,
        ),
        out_shape=[jax.ShapeDtypeStruct(s, d) for s, d in out_shapes],
        compiler_params=pltpu.CompilerParams(vmem_limit_bytes=56 * 1024 * 1024),
        cost_estimate=pl.CostEstimate(flops=int(us * 1.15e9), bytes_accessed=1 << 20, transcendentals=0),
    )(scalars, *args, *deps)


def whole(*shape):
    return pl.BlockSpec(shape, lambda i, s: (0,) * len(shape))


def part(*tail):
    return pl.BlockSpec((None,) + tail, lambda i, s: (i,) + (0,) * len(tail))


def near(*tail):
    return pl.BlockSpec((None,) + tail, lambda i, s: (jnp.maximum((i ^ s[0]) - 1, 0),) + (0,) * len(tail))


def rel(*tail):
    return pl.BlockSpec((None,) + tail, lambda i, s: (i ^ s[0],) + (0,) * len(tail))


def rel_out(*tail):
    return pl.BlockSpec((4, None) + tail, lambda i, s: (0, i ^ s[0]) + (0,) * len(tail))


def split_tail(v):
    value = v[16:24] + v[24:32]
    high = value.astype(BF16).astype(F32)
    return jnp.concatenate([v[0:16], high, value - high], 0).astype(BF16)


def sum_both_body(s, keep_x, keep_s, *refs):
    got_x, got_s, outs = refs[:4], refs[4], refs[5:]
    for m in range(4):
        outs[m][0:-TAIL_ROWS, :] = total([keep_x[m], got_x[m][...]]).astype(BF16)
        outs[m][-TAIL_ROWS:, :] = split_tail(total([keep_s[m], got_s[m]]))


def sum_both(place, keep_x, send_x, keep_s, send_s):
    zs, rows, cols = keep_x.shape[1:]
    shape = (zs, rows + TAIL_ROWS, cols)
    return call(
        sum_both_body,
        (zs,),
        [pl.BlockSpec((4, None, r, cols), lambda i, s: (0, i, 0, 0)) for r in (rows, TAIL_ROWS)]
        + [part(rows, cols)] * 4
        + [pl.BlockSpec((4, None, TAIL_ROWS, cols), lambda i, s: (0, i, 0, 0))],
        [part(rows + TAIL_ROWS, cols)] * 4,
        [(shape, BF16)] * 4,
        [],
        place,
        [keep_x, keep_s] + [swap(send_x[m], "dp", 1) for m in range(4)] + [swap(send_s, "dp", 1)],
    )


def plane_both_body(s, *refs):
    ins, outs = refs[:4], refs[4:]
    zs = len(outs)
    rows = ins[0].shape[1] - TAIL_ROWS
    for k in range(zs):
        outs[k][0:rows, :] = total([ref[k, 0:rows, :] for ref in ins]).astype(BF16)
    for k in range(zs):
        tail = split_tail(total([ref[k, rows:, :] for ref in ins]))
        at = rows + TAIL_ROWS * k
        for out in outs:
            out[at : at + TAIL_ROWS, :] = tail


def plane_both(place, halves, deps):
    zs, rows, cols = halves[0].shape
    out = (rows - TAIL_ROWS + zs * TAIL_ROWS, cols)
    return call(
        plane_both_body,
        (1,),
        [whole(zs, rows, cols)] * 4,
        [whole(*out)] * zs,
        [(out, BF16)] * zs,
        [],
        place,
        [halves[0]] + [swap(halves[m], "dp", 2 * m) for m in range(1, 4)],
        deps=deps,
    )


def line_both(place, quarter, deps):
    zs = len(quarter)
    rows, cols = quarter[0].shape
    first = rows - zs * TAIL_ROWS

    def body(s, *refs):
        ins, out = refs[:-1], refs[-1]
        out[0:first, :] = total([ref[0:first, :] for ref in ins]).astype(BF16)
        for b in range(zs):
            places = [first + TAIL_ROWS * (k ^ b) for k in range(zs)]
            parts = [ins[k][at : at + TAIL_ROWS, :] for k, at in enumerate(places)]
            at = first + TAIL_ROWS * b
            out[at : at + TAIL_ROWS, :] = split_tail(total(parts))

    def again(s, a, b, out):
        out[0:first, :] = total([a[0:first, :], b[0:first, :]]).astype(BF16)
        for at in range(first, rows, TAIL_ROWS):
            out[at : at + TAIL_ROWS, :] = split_tail(total([a[at : at + TAIL_ROWS, :], b[at : at + TAIL_ROWS, :]]))

    specs = [whole(rows, cols)]
    shape = [((rows, cols), BF16)]
    arrays = [quarter[0]] + [swap(q, "tensor", k) for k, q in enumerate(quarter) if k]
    mine = call(body, (1,), specs * zs, specs, shape, [], place, arrays, deps=deps)[0]
    bit = GROUP
    while bit < lax.axis_size("dp"):
        mine = call(again, (1,), specs * 2, specs, shape, [], place, [mine, swap(mine, "dp", bit)])[0]
        bit *= 2
    return mine


def plane_two_body(s, *refs):
    n = (len(refs) - 4) // 2
    ins, first, outs = refs[:4], refs[4 : 4 + n], refs[4 + n :]
    for k, out in enumerate(outs):
        out[0] = first[k][...]
        out[1] = total([ref[k] for ref in ins]).astype(out.dtype)


def plane_two(place, first, halves, deps):
    shape, dtype = halves[0].shape, halves[0].dtype
    return call(
        plane_two_body,
        (1,),
        [whole(*shape)] * 4 + [whole(*shape[1:])] * shape[0],
        [whole(2, *shape[1:])] * shape[0],
        [((2,) + shape[1:], dtype)] * shape[0],
        [],
        place,
        [halves[0]] + [swap(halves[m], "dp", 2 * m) for m in range(1, 4)] + list(first),
        deps=deps,
    )


def sum_pair_whole(place, keep, send, deps, us=4):
    zs, tail = keep.shape[1], keep.shape[2:]
    zeros = (0,) * len(tail)
    both = pl.BlockSpec((4, None) + tail, lambda i, s: (0, i) + zeros)

    def body(s, keep, got, *outs):
        for m in range(4):
            outs[m][...] = total([keep[m], got[m]]).astype(keep.dtype)

    return call(
        body,
        (zs,),
        [both] * 2,
        [part(*tail)] * 4,
        [((zs,) + tail, keep.dtype)] * 4,
        [],
        place,
        [keep, swap(send, "dp", 1)],
        us=us,
        deps=deps,
    )


def sum_plane_body(s, *refs):
    ins, outs = refs[:4], refs[4:]
    for k, out in enumerate(outs):
        out[...] = total([ref[k] for ref in ins]).astype(out.dtype)


def sum_plane(place, halves, deps):
    shape, dtype = halves[0].shape, halves[0].dtype
    return call(
        sum_plane_body,
        (1,),
        [whole(*shape)] * 4,
        [whole(*shape[1:])] * shape[0],
        [(shape[1:], dtype)] * shape[0],
        [],
        place,
        [halves[0]] + [swap(halves[m], "dp", 2 * m) for m in range(1, 4)],
        deps=deps,
    )


def sum_all_body(s, *refs):
    refs[-1][...] = total([ref[...] for ref in refs[:-1]]).astype(refs[-1].dtype)


def sum_all(place, arrays, deps):
    shape, dtype = arrays[0].shape, arrays[0].dtype
    specs = [whole(*shape)]
    return call(
        sum_all_body, (1,), specs * len(arrays), specs, [(shape, dtype)], [], place, arrays, deps=deps
    )[0]


def sum_line(place, quarter, deps):
    ds = lax.axis_size("dp")
    mine = sum_all(place, [quarter[0]] + [swap(q, "tensor", k) for k, q in enumerate(quarter) if k], deps)
    bit = GROUP
    while bit < ds:
        mine = sum_all(place, [mine, swap(mine, "dp", bit)], [])
        bit *= 2
    return mine


def assemble(s, own, pieces, out):
    i = pl.program_id(0)
    rows = pieces[0].shape[0]

    @pl.when(i == s[0])
    def _():
        out[...] = own[...]

    @pl.when(i != s[0])
    def _():
        for n in range(GROUP):
            place = pl.multiple_of((s[1] ^ n) * rows, rows)
            out[pl.ds(place, rows), :] = pieces[n][...]


def split_rows(s, full, keep, send):
    rows = full.shape[0] // GROUP
    for n in range(GROUP):
        place = pl.multiple_of((s[1] ^ n) * rows, rows)
        value = full[pl.ds(place, rows), :].astype(BF16)
        if n & 1 and len(send) == 1:
            send[0][n >> 1] = value
        elif n & 1:
            send[n >> 1][...] = value
        else:
            keep[n >> 1] = value


def iota(shape, dim):
    return lax.broadcasted_iota(jnp.int32, shape, dim)


def spread_sel(n, width, p):
    shape = (2 * LANES, width)
    return (iota(shape, 0) % LANES == iota(shape, 1) // p + n * SLOT).astype(BF16)


def gather_sel(n, width, p):
    shape = (width, LANES)
    return (iota(shape, 0) // p + n * SLOT == iota(shape, 1)).astype(BF16)


def head_lanes(heads, width, p):
    shape = (heads, width)
    return (iota(shape, 1) // p == iota(shape, 0)).astype(F32)


def flat_lanes(heads, width, first):
    shape = (heads, width)
    return (iota(shape, 1) == iota(shape, 0) + first).astype(F32)


def sigmoid(v):
    return 1.0 / (1.0 + jnp.exp(-v))


def softplus(v):
    return jnp.maximum(v, 0.0) + jnp.log1p(jnp.exp(-jnp.abs(v)))


def exact_sum(v, ones):
    a = v.astype(BF16)
    rest = v - a.astype(F32)
    b = rest.astype(BF16)
    c = (rest - b.astype(F32)).astype(BF16)
    return mm(a, ones) + mm(b, ones) + mm(c, ones)


def conv_rows(src, weight, bias, masks, count):
    taps = weight.shape[0]
    acc = bias + weight[taps - 1 : taps, :] * src[HALO : HALO + count, :]
    for j in range(1, taps):
        moved = src[HALO - j : HALO - j + count, :] * masks[:, j : j + 1]
        acc = acc + weight[taps - 1 - j : taps - j, :] * moved
    return acc


def conv_rows_back(pad, weight, masks_b, rows):
    taps = weight.shape[0]
    acc = weight[taps - 1 : taps, :] * pad[0:rows, :]
    for j in range(1, taps):
        acc = acc + weight[taps - 1 - j : taps - j, :] * (pad[j : j + rows, :] * masks_b[:, j : j + 1])
    return jnp.concatenate([acc[HALO:], acc[:HALO]], 0)


def slope(v):
    sig = sigmoid(v)
    return sig * (1.0 + v * (1.0 - sig))


def same_doc(dcol, drow, b, causal):
    shape = (CH, CH)
    column = dcol[HALO + b * CH : HALO + (b + 1) * CH, :]
    row = drow[:, b * CH : (b + 1) * CH]
    order = iota(shape, 0) >= iota(shape, 1) if causal else iota(shape, 0) <= iota(shape, 1)
    return (column == row) & order


def norm_body(s, hid, halo, gain, dcol, drow, w_bc, cw, cb,
              nx_o, inv_o, masks_o, masks_b_o, raw_o, bm_o, cm_o, bm_t_o, cm_t_o, gram_o, gram_t_o, scr):
    count = hid.shape[0]
    rows = HALO + count
    taps = cw.shape[0]
    n = bm_o.shape[1]
    ext = jnp.concatenate([hid[...], halo[...]], 0).astype(F32)
    inv = lax.rsqrt(jnp.mean(ext * ext, -1, keepdims=True) + epsilon)
    inv_o[...] = inv
    nx_o[...] = (ext * inv * gain[...]).astype(BF16)
    raw = mm(nx_o[...], w_bc[...])
    scr[0:HALO, :] = raw[count:]
    scr[HALO:, :] = raw[:count]
    raw_o[...] = scr[...]
    masks_o[...] = jnp.ones_like(masks_o)
    masks_b_o[...] = jnp.ones_like(masks_b_o)
    for j in range(1, taps):
        masks_o[:, j : j + 1] = (dcol[HALO - j : rows - j, :] == dcol[HALO:rows, :]).astype(F32)
        masks_b_o[:, j : j + 1] = (dcol[j : rows + j, :] == dcol[0:rows, :]).astype(F32)
    pre = conv_rows(scr, cw[...], cb[...], masks_o[...], count)
    states = pre * sigmoid(pre)
    flipped = states.T
    bm_o[...] = states[:, :n].astype(BF16)
    cm_o[...] = states[:, n:].astype(BF16)
    bm_t_o[...] = flipped[:n].astype(BF16)
    cm_t_o[...] = flipped[n:].astype(BF16)
    for b in range(count // CH):
        t = slice(b * CH, (b + 1) * CH)
        gram_o[b] = jnp.where(same_doc(dcol, drow, b, True), mm_nt(cm_o[t, :], bm_o[t, :]), 0.0)
        gram_t_o[b] = jnp.where(same_doc(dcol, drow, b, False), mm_nt(bm_o[t, :], cm_o[t, :]), 0.0)


def heads_body(s, pack, nx, dcol, drow, cum_o, pre_o, cols_o, parts_o, kap_o, dev_o, scr):
    heads, count = cum_o.shape
    width = pack.shape[1]
    p = width // heads
    flat = pack[FLAT : FLAT + 1, :]
    bias = jnp.sum(flat * flat_lanes(heads, width, 0), 1, keepdims=True)
    rate = -jnp.exp(jnp.sum(flat * flat_lanes(heads, width, heads), 1, keepdims=True))
    pre = bias
    for ch in range(nx.shape[1] // width):
        w = pack[W_DT + ch * heads : W_DT + (ch + 1) * heads, :].astype(BF16)
        pre = pre + mm_nt(w, nx[0:count, ch * width : (ch + 1) * width])
    pre_o[...] = pre
    step = softplus(pre)
    log_decay = step * rate
    ones = (iota((CH, CH), 0) <= iota((CH, CH), 1)).astype(BF16)
    spread = head_lanes(heads, width, p)
    scr[...] = jnp.zeros_like(scr)
    dev = None
    for b in range(count // CH):
        t = slice(b * CH, (b + 1) * CH)
        cum = exact_sum(log_decay[:, t], ones)
        cum_o[:, t] = cum
        end = cum[:, CH - 1 : CH]
        docs = drow[:, t]
        prev = dcol[HALO + b * CH - 1 : HALO + b * CH, :]
        last = dcol[HALO + (b + 1) * CH - 1 : HALO + (b + 1) * CH, :]
        fade = jnp.exp(end - cum) * (docs == last).astype(F32)
        for n, value in ((CUM, cum), (STEP, step[:, t]), (FADE, fade), (TAIL, fade * step[:, t]),
                         (HEAD, jnp.exp(cum) * (docs == prev).astype(F32))):
            scr[n * SLOT : n * SLOT + heads, t] = value
        kap = jnp.sum(jnp.exp(end) * (last == prev).astype(F32) * spread, 0, keepdims=True)
        kap_o[b : b + 1, :] = kap
        dev = kap if dev is None else dev * kap
    dev_o[...] = dev
    cols = scr[...].T
    cols_o[...] = cols
    high = cols.astype(BF16)
    parts_o[:, :LANES] = high
    parts_o[:, LANES:] = (cols - high.astype(F32)).astype(BF16)


def value_body(s, nx, own, *refs):
    pieces, (pack, masks, cols, b_t, kap, w_o, raw_o, xs_o, slope_o, e_o, dev_o, scr) = refs[:GROUP], refs[GROUP:]
    assemble(s, own, pieces, w_o)
    count, width = xs_o.shape
    taps = CONV_B
    raw = mm(nx[...], w_o[...])
    scr[0:HALO, :] = raw[count:]
    scr[HALO:, :] = raw[:count]
    raw_o[...] = scr[...].astype(BF16)
    pre = conv_rows(scr, pack[0:taps, :], pack[CONV_B : CONV_B + 1, :], masks[...], count)
    sig = sigmoid(pre)
    xs = pre * sig
    xs_o[...] = xs.astype(BF16)
    slope_o[...] = (sig * (1.0 + pre * (1.0 - sig))).astype(BF16)
    scaled = (xs * mm(cols[...], spread_sel(TAIL, width, HEAD_DIM))).astype(BF16)
    last = None
    for b in range(count // CH):
        fresh = mm(b_t[:, b * CH : (b + 1) * CH], scaled[b * CH : (b + 1) * CH])
        e_o[b] = fresh
        last = fresh if last is None else kap[b : b + 1, :] * last + fresh
    dev_o[...] = last.astype(BF16)


def gates_body(s, nx, cot, own, *refs):
    pieces, (wz_o, wo_o, z_o, d_o) = refs[:GROUP], refs[GROUP:]
    assemble(s, own.at[0], [ref.at[0] for ref in pieces], wz_o)
    assemble(s, own.at[1], [ref.at[1] for ref in pieces], wo_o)
    count, width = z_o.shape
    z_o[...] = mm(nx[0:count, :], wz_o[...]).astype(BF16)
    acc = None
    for ch in range(cot.shape[1] // width):
        c = slice(ch * width, (ch + 1) * width)
        term = mm_nt(cot[:, c], wo_o[c, :])
        acc = term if acc is None else acc + term
    d_o[...] = acc.astype(BF16)


def intra_body(s, xs, gram, cols, row, parts, pack, y_o):
    count, width = xs.shape
    heads = row.shape[0]
    p = width // heads
    x32 = xs[...].astype(F32)
    inputs = (x32 * mm(parts[...], spread_sel(STEP, width, p))).astype(BF16)
    left = iota((CH, 2 * p), 1) < p
    skip = pack[SKIP : SKIP + 1, :]
    for b in range(count // CH):
        t = slice(b * CH, (b + 1) * CH)
        a = gram[b]
        for pair in range(heads // 2):
            lanes = slice(2 * p * pair, 2 * p * (pair + 1))
            outs = []
            for h in (2 * pair, 2 * pair + 1):
                arg = jnp.minimum(cols[t, CUM * SLOT + h : CUM * SLOT + h + 1] - row[h : h + 1, t], 0.0)
                outs.append(mm((jnp.exp(arg) * a).astype(BF16), inputs[t, lanes]))
            y_o[t, lanes] = jnp.where(left, outs[0], outs[1]) + skip[:, lanes] * x32[t, lanes]


def carry_body(s, intra, cm, parts, e, kap, z_in, d_in, pack, *refs):
    parts_in, (y_o, state_o, sq_o, dot_o) = refs[:-4], refs[-4:]
    count, width = intra.shape
    scale = mm(parts[...], spread_sel(HEAD, width, HEAD_DIM))
    state = total([ref[...] for ref in parts_in])
    gain = pack[GAIN : GAIN + 1, :]

    @pl.when(pl.program_id(0) == 0)
    def _():
        sq_o[...] = jnp.zeros_like(sq_o)
        dot_o[...] = jnp.zeros_like(dot_o)

    for b in range(count // CH):
        t = slice(b * CH, (b + 1) * CH)
        low = state.astype(BF16)
        state_o[b] = low
        y = intra[t, :] + mm(cm[t, :], low) * scale[t]
        y_o[t, :] = y.astype(BF16)
        state = kap[b : b + 1, :] * state + e[b]
        z = z_in[t, :].astype(F32)
        gated = y * (z * sigmoid(z))
        sq = gated * gated
        dot = d_in[t, :].astype(F32) * gain * gated
        for lane in range(0, width, LANES):
            sq_o[t, :] += sq[:, lane : lane + LANES]
            dot_o[t, :] += dot[:, lane : lane + LANES]


def gate_back_body(s, y_in, z_in, d_in, pack, sq, dots, parts, c_t, kap, ng_o, dy_o, dz_o, gg_o, g_o, dev_o):
    count, width = y_in.shape
    channels = width * pl.num_programs(0)
    inv = lax.rsqrt(jnp.sum(sq[...], 1, keepdims=True) / channels + epsilon)
    coef = inv * inv * inv * (jnp.sum(dots[...], 1, keepdims=True) / channels)
    scale = mm(parts[...], spread_sel(HEAD, width, HEAD_DIM))
    gain = pack[GAIN : GAIN + 1, :]
    y = y_in[...].astype(F32)
    z = z_in[...].astype(F32)
    d_gate = d_in[...].astype(F32)
    sig = sigmoid(z)
    act = z * sig
    gated = y * act
    normed = gated * inv
    ng_o[...] = (normed * gain).astype(BF16)
    gg_o[...] = jnp.sum(d_gate * normed, 0, keepdims=True)
    d_gated = inv * (d_gate * gain) - gated * coef
    dy = d_gated * act
    dy_o[...] = dy.astype(BF16)
    dz_o[...] = (d_gated * y * (sig * (1.0 + z * (1.0 - sig)))).astype(BF16)
    scaled = (dy * scale).astype(BF16)
    back = None
    for b in reversed(range(count // CH)):
        t = slice(b * CH, (b + 1) * CH)
        fresh = mm(c_t[:, t], scaled[t])
        g_o[b] = fresh
        back = fresh if back is None else fresh + kap[b : b + 1, :] * back
    dev_o[...] = back.astype(BF16)


def out_body(s, ng, wo, cot, hid, keep, *refs):
    send, (out_o, acc, scr) = refs[:1], refs[1:]
    i = pl.program_id(0)
    width = ng.shape[1]

    @pl.when(i == 0)
    def _():
        acc[...] = hid[...].astype(F32)

    for ch in range(hid.shape[1] // width):
        c = slice(ch * width, (ch + 1) * width)
        acc[:, c] += mm(ng[...], wo[c, :])
        scr[c, :] = mm_tn(ng[...], cot[:, c])
    split_rows(s, scr, keep, send)

    @pl.when(i == pl.num_programs(0) - 1)
    def _():
        out_o[...] = acc[...].astype(BF16)


def gate_grad_body(s, dz, wz, nx_t, keep, *refs):
    send, (dn_o, scr) = refs[:1], refs[1:]

    @pl.when(pl.program_id(0) == 0)
    def _():
        dn_o[...] = jnp.zeros_like(dn_o)

    dn_o[...] += mm_nt(dz[...], wz[...])
    scr[...] = mm(nx_t[:, 0 : dz.shape[0]], dz[...])
    split_rows(s, scr, keep, send)


def intra_back_body(s, xs, dy, gram_t, cols, row, parts, du_o, col_o, row_o, dg_o):
    count, width = xs.shape
    heads = row.shape[0]
    p = width // heads
    inputs = (xs[...].astype(F32) * mm(parts[...], spread_sel(STEP, width, p))).astype(BF16)
    left = iota((CH, 2 * p), 1) < p
    zero = jnp.zeros((CH, 2 * p), BF16)
    col_o[...] = jnp.zeros_like(col_o)

    @pl.when(pl.program_id(0) == 0)
    def _():
        dg_o[...] = jnp.zeros_like(dg_o)

    for b in range(count // CH):
        t = slice(b * CH, (b + 1) * CH)
        a = gram_t[b]
        d_gram = None
        for pair in range(heads // 2):
            lanes = slice(2 * p * pair, 2 * p * (pair + 1))
            u_pair, dy_pair = inputs[t, lanes], dy[t, lanes]
            outs = []
            for n in (0, 1):
                h = 2 * pair + n
                u_one = jnp.where(left, u_pair, zero) if n == 0 else jnp.where(left, zero, u_pair)
                d_w = mm_nt(u_one, dy_pair)
                fade = jnp.exp(jnp.minimum(row[h : h + 1, t] - cols[t, CUM * SLOT + h : CUM * SLOT + h + 1], 0.0))
                w_t = fade * a
                moment = d_w * w_t
                d_gram = d_w * fade if d_gram is None else d_gram + d_w * fade
                lane = 3 * SLOT + h
                col_o[t, lane : lane + 1] = jnp.sum(moment, 1, keepdims=True)
                row_o[h : h + 1, t] = jnp.sum(moment, 0, keepdims=True)
                outs.append(mm(w_t.astype(BF16), dy_pair))
            du_o[t, lanes] = jnp.where(left, outs[0], outs[1])
        dg_o[b] += d_gram


def value_back_body(s, xs_in, dy_in, du_in, raw, slope_in, state, g, kap, parts, bm, cm, pack, masks, masks_b,
                    nx_t, w, *refs):
    parts_in, refs = refs[:-16], refs[-16:]
    keep, send, refs = refs[0], refs[1:5], refs[5:]
    dn_o, db_o, dc_o, hs_o, kg_o, sk_o, gc_o, scr, pad, full, dx = refs
    count, width = xs_in.shape
    p = HEAD_DIM
    taps = CONV_B
    cw = pack[0:taps, :]
    skip = pack[SKIP : SKIP + 1, :]

    @pl.when(pl.program_id(0) == 0)
    def _():
        dn_o[...] = jnp.zeros_like(dn_o)
        db_o[...] = jnp.zeros_like(db_o)
        dc_o[...] = jnp.zeros_like(dc_o)

    sums = [gather_sel(n, width, p) for n in range(3)]
    scr[...] = raw[...].astype(F32)
    pad[0:HALO, :] = jnp.zeros((HALO, width), F32)
    pad[HALO + count :, :] = jnp.zeros((HALO, width), F32)
    d_state = total([ref[...] for ref in parts_in])
    skip_sum = jnp.zeros((1, width), F32)
    for b in reversed(range(count // CH)):
        t = slice(b * CH, (b + 1) * CH)
        low = d_state.astype(BF16)
        xs = xs_in[t, :].astype(F32)
        dy = dy_in[t, :].astype(F32)
        scaled_x = (xs * mm(parts[t, :], spread_sel(TAIL, width, p))).astype(BF16)
        scaled_dy = (dy * mm(parts[t, :], spread_sel(HEAD, width, p))).astype(BF16)
        d_scaled = mm(bm[t, :], low)
        db_o[t, :] += mm_nt(scaled_x, low)
        dc_o[t, :] += mm_nt(scaled_dy, state[b])
        from_state = mm(cm[t, :], state[b]) * scaled_dy.astype(F32)
        to_state = d_scaled * scaled_x.astype(F32)
        kg_o[b : b + 1, :] = jnp.sum(d_state * state[b].astype(F32), 0, keepdims=True)
        du = du_in[t, :] + d_scaled * mm(parts[t, :], spread_sel(FADE, width, p))
        hs_o[t, :] = (
            mm(from_state.astype(BF16), sums[0])
            + mm(to_state.astype(BF16), sums[1])
            + mm((du * xs).astype(BF16), sums[2])
        )
        skip_sum = skip_sum + jnp.sum(dy * xs, 0, keepdims=True)
        d_xs = du * mm(parts[t, :], spread_sel(STEP, width, p)) + skip * dy
        pad[HALO + b * CH : HALO + (b + 1) * CH, :] = d_xs * slope_in[t, :].astype(F32)
        d_state = g[b] + kap[b : b + 1, :] * d_state
    sk_o[...] = skip_sum
    d_pre = pad[HALO : HALO + count, :]
    for j in range(taps):
        moved = scr[HALO - j : HALO - j + count, :] * d_pre
        if j:
            moved = moved * masks[:, j : j + 1]
        gc_o[taps - 1 - j : taps - j, :] = jnp.sum(moved, 0, keepdims=True)
    gc_o[taps : taps + 1, :] = jnp.sum(d_pre, 0, keepdims=True)
    dx[...] = conv_rows_back(pad, cw, masks_b, HALO + count).astype(BF16)
    dn_o[...] += mm_nt(dx[...], w[...])
    full[...] = mm(nx_t[...], dx[...])
    split_rows(s, full, keep, send)


def finish_body(s, pack, pre_dt, row_sums, col_sums, head_sums, kap, kap_sums, skip_sums, conv_sums, g_gain,
                d_gram_t, dcol, drow, bm, cm, db, dc, raw, cw, cb, masks, masks_b, nx, nx_t, w_bc, dn_x, dn_z,
                hid, halo, inv, keep, send, dn_o, gbc, blk, vec, ddt, wdt, scr, pad, small):
    i = pl.program_id(0)
    heads, count = pre_dt.shape
    rows = HALO + count
    width = pack.shape[1]
    dim = nx.shape[1]
    p = width // heads
    zs = pl.num_programs(0)
    n = bm.shape[1]
    taps = cw.shape[0]
    cols = 2 * n
    n_blocks = keep.shape[1]
    per_piece = gbc.shape[0] // (GROUP * n_blocks)
    half = cols * per_piece // width

    @pl.when(i == 0)
    def _():
        small[...] = jnp.zeros_like(small)
        ddt[...] = jnp.zeros_like(ddt)
        wdt[...] = jnp.zeros_like(wdt)
        vec[...] = jnp.zeros_like(vec)
        scr[...] = raw[...]
        pad[...] = jnp.zeros_like(pad)
        for b in range(count // CH):
            t = slice(b * CH, (b + 1) * CH)
            d_gram = jnp.where(same_doc(dcol, drow, b, False), d_gram_t[b], 0.0).astype(BF16)
            pad[HALO + b * CH : HALO + (b + 1) * CH, 0:n] = db[t, :] + mm(d_gram, cm[t, :])
            pad[HALO + b * CH : HALO + (b + 1) * CH, n:cols] = dc[t, :] + mm_tn(d_gram, bm[t, :])
        pre = conv_rows(scr, cw[...], cb[...], masks[...], count)
        d_pre = pad[HALO : HALO + count, :] * slope(pre)
        pad[HALO : HALO + count, :] = d_pre
        for j in range(taps):
            moved = scr[HALO - j : HALO - j + count, :] * d_pre
            if j:
                moved = moved * masks[:, j : j + 1]
            place = dim // cols + taps - 1 - j
            vec[place : place + 1, :] = jnp.sum(moved, 0, keepdims=True)
        place = dim // cols + taps
        vec[place : place + 1, :] = jnp.sum(d_pre, 0, keepdims=True)
        d_raw = conv_rows_back(pad, cw[...], masks_b[...], rows)
        high = d_raw.astype(BF16)
        low = (d_raw - high.astype(F32)).astype(BF16)
        gbc[...] = mm(nx_t[...], high) + mm(nx_t[...], low)
        dn_o[...] = dn_x[...] + mm_nt(high, w_bc[...]) + mm_nt(low, w_bc[...])
        dn_o[0:count, :] += dn_z[...]

    flat = pack[FLAT : FLAT + 1, :]
    rate = -jnp.exp(jnp.sum(flat * flat_lanes(heads, width, heads), 1, keepdims=True))
    pre = pre_dt[...]
    log_decay = softplus(pre) * rate
    sums = (head_sums[...] + col_sums[...]).T
    from_state = sums[0:heads]
    to_state = sums[SLOT : SLOT + heads]
    d_cum = row_sums[...] - sums[3 * SLOT : 3 * SLOT + heads] + from_state - to_state
    spread = head_lanes(heads, width, p)
    ones = (iota((CH, CH), 0) >= iota((CH, CH), 1)).astype(BF16)
    g_bias = jnp.zeros((heads, 1), F32)
    g_log = jnp.zeros((heads, 1), F32)
    place = pl.multiple_of(i * SLOT, SLOT)
    for b in range(count // CH):
        t = slice(b * CH, (b + 1) * CH)
        d_end = jnp.sum(to_state[:, t], 1, keepdims=True)
        d_end = d_end + jnp.sum(kap[b : b + 1, :] * kap_sums[b : b + 1, :] * spread, 1, keepdims=True)
        d_log = exact_sum(d_cum[:, t], ones) + d_end
        d_step = sums[2 * SLOT : 2 * SLOT + heads, t] + d_log * rate
        d_dt = d_step * sigmoid(pre[:, t])
        g_log = g_log + jnp.sum(d_log * log_decay[:, t], 1, keepdims=True)
        g_bias = g_bias + jnp.sum(d_dt, 1, keepdims=True)
        ddt[pl.ds(place, heads), t] = d_dt
    d_dt = ddt[pl.ds(place, heads), :].astype(BF16)

    def put(row, value):
        blk[row // 4, row % 4 : row % 4 + 1, :] = value

    blk[...] = jnp.zeros_like(blk)
    for r in range(taps + 1):
        put(r, conv_sums[r : r + 1, :])
    put(GAIN, g_gain[...])
    g_skip = jnp.sum(skip_sums[...] * spread, 1, keepdims=True)
    put(FLAT, jnp.sum(
        g_bias * flat_lanes(heads, width, 0)
        + g_log * flat_lanes(heads, width, heads)
        + g_skip * flat_lanes(heads, width, 2 * heads), 0, keepdims=True))
    for ch in range(dim // width):
        c = slice(ch * width, (ch + 1) * width)
        first = W_DT + ch * heads
        wdt[pl.ds(place, heads), c] = pack[first : first + heads, :]
        g_dt = mm(d_dt, nx[0:count, c])
        for h in range(heads):
            put(first + h, g_dt[h : h + 1, :])
    where = i ^ s[0]
    for m in range(GROUP):
        small[m, where, 16:20, :] = blk[s[1] ^ m, 0:4, :]

    @pl.when(i == zs - 1)
    def _():
        dn_o[0:count, :] += mm(ddt[...].T.astype(BF16), wdt[...].astype(BF16))
        weight_own = hid[...].astype(F32) * inv[0:count, :]
        weight_halo = halo[...].astype(F32) * inv[count:, :]
        g_norm = jnp.sum(dn_o[0:count, :] * weight_own, 0, keepdims=True)
        g_norm = g_norm + jnp.sum(dn_o[count:, :] * weight_halo, 0, keepdims=True)
        for c in range(dim // cols):
            vec[c : c + 1, :] = g_norm[:, c * cols : (c + 1) * cols]
        for m in range(GROUP):
            target = send if m & 1 else keep
            for k in range(n_blocks):
                at = (s[1] ^ m) * n_blocks + (k ^ s[0])
                for c in range(width // cols):
                    block = pl.multiple_of(at * per_piece + c * half, half)
                    small[m, k, 0:half, c * cols : (c + 1) * cols] = gbc[pl.ds(block, half), :]
                small[m, k, 20:21, 0:cols] = vec[pl.ds(at, 1), :]
                target[m >> 1, k] = split_tail(small[m, k])


def hidden_body(s, dn, later, hid, inv, gain, cot, out):
    count = hid.shape[0]

    def rows(t, d):
        scaled = d * gain[...]
        own = hid[t, :].astype(F32)
        r = inv[t, :]
        mean = jnp.mean(scaled * own, -1, keepdims=True)
        out[t, :] = cot[t, :].astype(F32) + r * scaled - own * (r * r * r * mean)

    rows(slice(0, count - HALO), dn[0 : count - HALO, :])
    rows(slice(count - HALO, count), dn[count - HALO : count, :] + later[...])


def scale_body(s, x, factor, out):
    out[...] = (x[...].astype(F32) * factor[...]).astype(BF16)


def join_two_body(s, *refs):
    pieces, (go, gz, scr) = refs[:GROUP], refs[GROUP:]
    rows, width = pieces[0].shape[1:]
    for n in range(GROUP):
        place = pl.multiple_of((s[1] ^ n) * rows, rows)
        scr[pl.ds(place, rows), :] = pieces[n][0].astype(F32)
        gz[pl.ds(place, rows), :] = pieces[n][1].astype(F32)
    for ch in range(go.shape[1] // width):
        c = slice(ch * width, (ch + 1) * width)
        go[:, c] = scr[c, :]


def join_all_body(s, *refs):
    pieces, (gx, gbc, blk, vec) = refs[:GROUP], refs[GROUP:]
    rows, width = gx.shape[0] // GROUP, gx.shape[1]
    cols = gbc.shape[1]
    zs = (pieces[0].shape[0] - rows) // TAIL_ROWS
    per_piece = gbc.shape[0] // (GROUP * zs)
    half = cols * per_piece // width
    for n in range(GROUP):
        a = s[1] ^ n
        gx[pl.ds(pl.multiple_of(a * rows, rows), rows), :] = pieces[n][0:rows, :].astype(F32)
        for k in range(zs):
            tail = pieces[n][rows + k * TAIL_ROWS : rows + (k + 1) * TAIL_ROWS, :].astype(F32)
            value = tail[16:24] + tail[24:32]
            at = a * zs + (k ^ s[0])
            if k == 0:
                blk[pl.ds(pl.multiple_of(a * SLOT, SLOT), SLOT), :] = value
            vec[pl.ds(pl.multiple_of(at * SLOT, SLOT), SLOT), :] = value
            for c in range(width // cols):
                block = pl.multiple_of(at * per_piece + c * half, half)
                gbc[pl.ds(block, half), :] = tail[0:half, c * cols : (c + 1) * cols]


def on_device(
    hidden,
    segment_ids,
    norm_gain,
    w_z,
    w_x,
    w_bc,
    w_dt,
    conv_x_w,
    conv_x_b,
    conv_bc_w,
    conv_bc_b,
    dt_bias,
    a_log,
    skip_d,
    gate_gain,
    w_out,
    cotangent,
):
    zs = lax.axis_size("tensor")
    z = lax.axis_index("tensor")
    piece_index = lax.axis_index("dp") & (GROUP - 1)
    place = jnp.stack([z, piece_index]).astype(jnp.int32)
    hid = hidden[0]
    cot = cotangent[0]
    count, dim = hid.shape
    taps, width = conv_x_w.shape
    heads = w_dt.shape[1]
    p = width // heads
    n = w_bc.shape[1] // 2
    blocks = count // CH
    rows = HALO + count
    chunks = dim // width
    wr = dim // GROUP

    got_x = gather_blocks(lax.dynamic_slice_in_dim(w_x, piece_index * wr, wr, 0))
    halo = shift_up(hid[count - HALO :], "tensor", 1)
    flat = jnp.concatenate([dt_bias, a_log, skip_d])
    by_chunk = w_dt.astype(F32).reshape(chunks, width, heads).transpose(0, 2, 1).reshape(chunks * heads, width)
    pack = jnp.concatenate(
        [
            conv_x_w,
            conv_x_b[None],
            gate_gain[None],
            jnp.repeat(skip_d, p)[None],
            jnp.pad(flat, (0, width - flat.shape[0]))[None],
            by_chunk,
        ],
        0,
    )
    pack = jnp.stack([pack] + [swap(pack, "tensor", k) for k in range(1, zs)], 0)
    out_chunks = w_out.reshape(width, chunks, width).transpose(1, 0, 2).reshape(dim, width)
    two = jnp.stack([w_z, out_chunks], 0)
    got_two = gather_blocks(lax.dynamic_slice_in_dim(two, piece_index * wr, wr, 1))
    x_pieces = spread_pieces(got_x)
    two_pieces = spread_pieces(got_two)

    docs = segment_ids[0].astype(F32)
    padded = jnp.concatenate([jnp.full((HALO,), -1.0, F32), docs])
    ext = lax.dynamic_slice_in_dim(padded, z * count, rows, 0)
    dcol = jnp.concatenate([ext, jnp.full((HALO,), -2.0, F32)])[:, None]
    drow = ext[None, HALO:]

    state_spec = part(blocks, n, width)
    dev_spec = part(n, width)
    wide = part(count, width)
    vec = part(1, width)
    kap_spec = part(blocks, width)
    gram_spec = whole(blocks, CH, CH)
    token_state = whole(count, n)
    state_token = whole(n, count)
    dcol_spec, drow_spec = whole(rows + HALO, 1), whole(1, count)
    mask_specs = [whole(count, SLOT), whole(rows, SLOT)]
    pack_spec = rel(pack.shape[1], width)
    parts_spec, cols_spec = part(count, 2 * LANES), part(count, LANES)
    row_spec = part(heads, count)
    bcw_specs = [whole(taps, 2 * n), whole(1, 2 * n)]
    big = (zs, count, width)
    states_shape = (zs, blocks, n, width)
    gain_row = norm_gain[None]
    cb_row = conv_bc_b[None]

    nx, inv, masks, masks_b, bc_raw, bm, cm, bm_t, cm_t, gram, gram_t = call(
        norm_body,
        (1,),
        [whole(count, dim), whole(HALO, dim), whole(1, dim), dcol_spec, drow_spec, whole(dim, 2 * n)] + bcw_specs,
        [whole(rows, dim), whole(rows, 1)]
        + mask_specs
        + [whole(rows, 2 * n), token_state, token_state, state_token, state_token, gram_spec, gram_spec],
        [
            ((rows, dim), BF16),
            ((rows, 1), F32),
            ((count, SLOT), F32),
            ((rows, SLOT), F32),
            ((rows, 2 * n), F32),
            ((count, n), BF16),
            ((count, n), BF16),
            ((n, count), BF16),
            ((n, count), BF16),
            ((blocks, CH, CH), F32),
            ((blocks, CH, CH), F32),
        ],
        [pltpu.VMEM((rows, 2 * n), F32)],
        place,
        [hid, halo, gain_row, dcol, drow, w_bc, conv_bc_w, cb_row],
        us=6,
        deps=[got_x],
    )
    nx_t = nx.T
    cum, pre_dt, cols, parts, kap, kap_dev = call(
        heads_body,
        (zs,),
        [pack_spec, whole(rows, dim), dcol_spec, drow_spec],
        [row_spec, row_spec, cols_spec, parts_spec, kap_spec, vec],
        [
            ((zs, heads, count), F32),
            ((zs, heads, count), F32),
            ((zs, count, LANES), F32),
            ((zs, count, 2 * LANES), BF16),
            ((zs, blocks, width), F32),
            ((zs, 1, width), F32),
        ],
        [pltpu.VMEM((LANES, count), F32)],
        place,
        [pack, nx, dcol, drow],
        us=4,
    )
    wx, raw, xs, slopes, e, dev = call(
        value_body,
        (zs,),
        [whole(rows, dim), whole(dim, width)]
        + [near(wr, width)] * GROUP
        + [pack_spec, mask_specs[0], parts_spec, state_token, kap_spec],
        [part(dim, width), part(rows, width), wide, wide, state_spec, dev_spec],
        [
            ((zs, dim, width), BF16),
            ((zs, rows, width), BF16),
            (big, BF16),
            (big, BF16),
            (states_shape, F32),
            ((zs, n, width), BF16),
        ],
        [pltpu.VMEM((rows, width), F32)],
        place,
        [nx, w_x, *x_pieces, pack, masks, parts, bm_t, kap],
        us=12,
    )

    steps = min(zs - 1, (DOC_MAX - 2) // count + 1)

    def pass_on(message, by, deps):
        got = []
        for k in range(steps):
            got.append(shift_up(message, "tensor", by))
            if k + 1 < steps:
                message = call(
                    scale_body, (1,), [whole(zs, n, width), whole(zs, 1, width)], [whole(zs, n, width)],
                    [((zs, n, width), BF16)], [], place, [got[-1], kap_dev], us=0.3, deps=deps,
                )[0]
        return got, message

    intra = call(
        intra_body,
        (zs,),
        [wide, gram_spec, cols_spec, row_spec, parts_spec, pack_spec],
        [wide],
        [(big, F32)],
        [],
        place,
        [xs, gram, cols, cum, parts, pack],
        us=8,
    )[0]
    carried, scaled = pass_on(dev, 1, [intra])
    wz, wo, z_raw, d_gate = call(
        gates_body,
        (zs,),
        [whole(rows, dim), whole(count, dim), whole(2, dim, width)] + [near(2, wr, width)] * GROUP,
        [part(dim, width), part(dim, width), wide, wide],
        [((zs, dim, width), BF16), ((zs, dim, width), BF16), (big, BF16), (big, BF16)],
        [],
        place,
        [nx, cot, two, *two_pieces],
        us=14,
        deps=[scaled],
    )
    lanes = whole(count, LANES)
    y, state, squares, dots = call(
        carry_body,
        (zs,),
        [wide, token_state, parts_spec, state_spec, kap_spec, wide, wide, pack_spec] + [dev_spec] * steps,
        [wide, state_spec, lanes, lanes],
        [(big, BF16), (states_shape, BF16), ((count, LANES), F32), ((count, LANES), F32)],
        [],
        place,
        [intra, cm, parts, e, kap, z_raw, d_gate, pack, *carried],
        us=9,
    )
    ng, dy, dz, g_gain, g_state, g_dev = call(
        gate_back_body,
        (zs,),
        [wide, wide, wide, pack_spec, lanes, lanes, parts_spec, state_token, kap_spec],
        [wide, wide, wide, vec, state_spec, dev_spec],
        [(big, BF16)] * 3 + [((zs, 1, width), F32), (states_shape, F32), ((zs, n, width), BF16)],
        [],
        place,
        [y, z_raw, d_gate, pack, squares, dots, parts, cm_t, kap],
        us=10,
    )
    grad_specs = [rel_out(wr, width)] + [rel(wr, width)] * 4
    grad_shapes = [((4, zs, wr, width), BF16)] + [((zs, wr, width), BF16)] * 4
    keep_o, send_o, block_out = call(
        out_body,
        (zs,),
        [wide, part(dim, width), whole(count, dim), whole(count, dim)],
        [rel_out(wr, width)] * 2 + [whole(count, dim)],
        grad_shapes[:1] * 2 + [((count, dim), BF16)],
        [pltpu.VMEM((count, dim), F32), pltpu.VMEM((dim, width), F32)],
        place,
        [ng, wo, cot, hid],
        us=10,
    )
    keep_z, send_z, dn_z = call(
        gate_grad_body,
        (zs,),
        [wide, part(dim, width), whole(dim, rows)],
        [rel_out(wr, width)] * 2 + [whole(count, dim)],
        grad_shapes[:1] * 2 + [((count, dim), F32)],
        [pltpu.VMEM((dim, width), F32)],
        place,
        [dz, wz, nx_t],
        us=10,
        deps=[keep_o],
    )
    halves_o = sum_pair_whole(place, keep_o, send_o, [keep_z])
    from_later, scaled = pass_on(g_dev, -1, [halves_o[0]])
    du, col_sums, row_sums, d_gram_t = call(
        intra_back_body,
        (zs,),
        [wide, wide, gram_spec, cols_spec, row_spec, parts_spec],
        [wide, cols_spec, row_spec, gram_spec],
        [(big, F32), ((zs, count, LANES), F32), ((zs, heads, count), F32), ((blocks, CH, CH), F32)],
        [],
        place,
        [xs, dy, gram_t, cols, cum, parts],
        us=17,
        deps=[scaled],
    )
    halves_z = sum_pair_whole(place, keep_z, send_z, [du])
    quarter_o = sum_plane(place, halves_o, [halves_z[0]])
    keep_x, *send_x, dn_x, db, dc, head_sums, kap_sums, skip_sums, conv_sums = call(
        value_back_body,
        (zs,),
        [wide] * 3
        + [part(rows, width), wide, state_spec, state_spec, kap_spec, parts_spec, token_state, token_state]
        + [pack_spec]
        + mask_specs
        + [whole(dim, rows), part(dim, width)]
        + [dev_spec] * steps,
        grad_specs
        + [whole(rows, dim), token_state, token_state]
        + [cols_spec, kap_spec, vec, part(taps + 1, width)],
        grad_shapes
        + [
            ((rows, dim), F32),
            ((count, n), F32),
            ((count, n), F32),
            ((zs, count, LANES), F32),
            ((zs, blocks, width), F32),
            ((zs, 1, width), F32),
            ((zs, taps + 1, width), F32),
        ],
        [
            pltpu.VMEM((rows, width), F32),
            pltpu.VMEM((rows + HALO, width), F32),
            pltpu.VMEM((dim, width), F32),
            pltpu.VMEM((rows, width), BF16),
        ],
        place,
        [xs, dy, du, raw, slopes, state, g_state, kap, parts, bm, cm, pack, masks, masks_b, nx_t, wx, *from_later],
        us=28,
        deps=[quarter_o[0], halves_z[0]],
    )
    quarter_two = plane_two(place, quarter_o, halves_z, [dn_x])

    keep_s, send_s, dn = call(
        finish_body,
        (zs,),
        [pack_spec, row_spec, row_spec, cols_spec, cols_spec, kap_spec, kap_spec, vec, part(taps + 1, width), vec]
        + [gram_spec, dcol_spec, drow_spec] + [token_state] * 4 + [whole(rows, 2 * n)] + bcw_specs + mask_specs
        + [whole(rows, dim), whole(dim, rows), whole(dim, 2 * n), whole(rows, dim), whole(count, dim)]
        + [whole(count, dim), whole(HALO, dim), whole(rows, 1)],
        [whole(4, zs, TAIL_ROWS, width)] * 2 + [whole(rows, dim)],
        [((4, zs, TAIL_ROWS, width), BF16)] * 2 + [((rows, dim), F32)],
        [
            pltpu.VMEM((dim, 2 * n), F32),
            pltpu.VMEM((GROUP, SLOT, width), F32),
            pltpu.VMEM((GROUP * zs, 2 * n), F32),
            pltpu.VMEM((LANES, count), F32),
            pltpu.VMEM((LANES, dim), F32),
            pltpu.VMEM((rows, 2 * n), F32),
            pltpu.VMEM((rows + HALO, 2 * n), F32),
            pltpu.VMEM((GROUP, zs, TAIL_ROWS, width), F32),
        ],
        place,
        [pack, pre_dt, row_sums, col_sums, head_sums, kap, kap_sums, skip_sums, conv_sums, g_gain]
        + [d_gram_t, dcol, drow, bm, cm, db, dc, bc_raw, conv_bc_w, cb_row, masks, masks_b]
        + [nx, nx_t, w_bc, dn_x, dn_z, hid, halo, inv],
        us=13,
        deps=[quarter_two[0]],
    )
    halves = sum_both(place, keep_x, send_x, keep_s, send_s)
    dn_later = shift_up(dn[count:], "tensor", -1)
    grad_hidden = call(
        hidden_body,
        (1,),
        [whole(rows, dim), whole(HALO, dim), whole(count, dim), whole(rows, 1), whole(1, dim), whole(count, dim)],
        [whole(count, dim)],
        [((count, dim), F32)],
        [],
        place,
        [dn, dn_later, hid, inv, gain_row, cot],
        us=0.3,
        deps=[halves[0]],
    )[0]
    quarter = plane_both(place, halves, [grad_hidden])
    mine_two = sum_line(place, quarter_two, [quarter[0]])
    mine = line_both(place, quarter, [mine_two])
    two_out = spread_pieces(mine_two)
    all_out = spread_pieces(mine)
    g_w_out, g_w_z = call(
        join_two_body,
        (1,),
        [whole(2, wr, width)] * GROUP,
        [whole(width, dim), whole(dim, width)],
        [((width, dim), F32), ((dim, width), F32)],
        [pltpu.VMEM((dim, width), F32)],
        place,
        two_out,
    )
    g_w_x, g_w_bc, blk, vec_rows = call(
        join_all_body,
        (1,),
        [whole(*mine.shape)] * GROUP,
        [whole(dim, width), whole(dim, 2 * n), whole(GROUP * SLOT, width), whole(GROUP * zs * SLOT, width)],
        [((dim, width), F32), ((dim, 2 * n), F32), ((GROUP * SLOT, width), F32), ((GROUP * zs * SLOT, width), F32)],
        [],
        place,
        all_out,
    )
    blocked = blk.reshape(GROUP, SLOT, width)[:, :4].reshape(4 * GROUP, width)
    vecs = vec_rows.reshape(GROUP * zs, SLOT, width)[:, 4, : 2 * n]
    flat = blocked[FLAT]
    g_w_dt = blocked[W_DT : W_DT + chunks * heads].reshape(chunks, heads, width).transpose(0, 2, 1).reshape(dim, heads)
    lead = dim // (2 * n)
    return (
        block_out[None],
        grad_hidden[None],
        vecs[:lead].reshape(dim),
        g_w_z,
        g_w_x,
        g_w_bc,
        g_w_dt,
        blocked[:taps],
        blocked[taps],
        vecs[lead : lead + taps],
        vecs[lead + taps],
        flat[:heads],
        flat[heads : 2 * heads],
        flat[2 * heads : 3 * heads],
        blocked[GAIN],
        g_w_out,
    )


def solution(mesh):
    placed = (
        P("dp", "tensor", None),
        P("dp", None),
        P(),
        P(None, "tensor"),
        P(None, "tensor"),
        P(),
        P(None, "tensor"),
        P(None, "tensor"),
        P("tensor"),
        P(),
        P(),
        P("tensor"),
        P("tensor"),
        P("tensor"),
        P("tensor"),
        P("tensor", None),
        P("dp", "tensor", None),
    )
    return jax.shard_map(
        on_device,
        mesh=mesh,
        in_specs=placed,
        out_specs=(
            P("dp", "tensor", None),
            P("dp", "tensor", None),
            P(),
            P(None, "tensor"),
            P(None, "tensor"),
            P(),
            P(None, "tensor"),
            P(None, "tensor"),
            P("tensor"),
            P(),
            P(),
            P("tensor"),
            P("tensor"),
            P("tensor"),
            P("tensor"),
            P("tensor", None),
        ),
        check_vma=False,
    )
```

```python
import jax
import jax.numpy as jnp
from jax import lax
from jax.experimental import pallas as pl
from jax.experimental.pallas import tpu as pltpu
from jax.sharding import PartitionSpec as P

CH = 256
HALO = 16
DOC_MAX = 1024
GROUP = 8
SLOT = 8
LANES = 128
TAIL_ROWS = 32
HEAD_DIM = 64
epsilon = 1e-05
F32 = jnp.float32
BF16 = jnp.bfloat16
CUM, STEP, FADE, TAIL, HEAD = range(5)
CONV_B, GAIN, SKIP, FLAT, W_DT = 4, 5, 6, 7, 8


def mm(a, b):
    return jnp.dot(a, b, preferred_element_type=F32)


def mm_nt(a, b):
    return lax.dot_general(a, b, (((1,), (1,)), ((), ())), preferred_element_type=F32)


def mm_tn(a, b):
    return lax.dot_general(a, b, (((0,), (0,)), ((), ())), preferred_element_type=F32)


def swap(x, axis, k):
    n = lax.axis_size(axis)
    return lax.ppermute(x, axis, [(i, i ^ k) for i in range(n)])


def shift_up(x, axis, by):
    n = lax.axis_size(axis)
    return lax.ppermute(x, axis, [(i, i + by) for i in range(n) if 0 <= i + by < n])


def gather_blocks(mine):
    zs = lax.axis_size("tensor")
    return jnp.stack([swap(mine, "tensor", k) for k in range(1, zs)], 0)


def spread_pieces(got):
    even = [got] + [swap(got, "dp", m) for m in (2, 4, 6)]
    pieces = []
    for part in even:
        pieces += [part, swap(part, "dp", 1)]
    return pieces


def total(parts):
    acc = parts[0].astype(F32)
    for part in parts[1:]:
        acc = acc + part.astype(F32)
    return acc


def call(body, grid, in_specs, out_specs, out_shapes, scratch, scalars, args, us=0.3, deps=()):
    n_in, n_deps = len(args), len(deps)

    def run(s, *refs):
        body(s, *refs[:n_in], *refs[n_in + n_deps :])

    return pl.pallas_call(
        run,
        grid_spec=pltpu.PrefetchScalarGridSpec(
            num_scalar_prefetch=1,
            grid=grid,
            in_specs=list(in_specs) + [pl.BlockSpec(memory_space=pl.ANY)] * n_deps,
            out_specs=out_specs,
            scratch_shapes=scratch,
        ),
        out_shape=[jax.ShapeDtypeStruct(s, d) for s, d in out_shapes],
        compiler_params=pltpu.CompilerParams(vmem_limit_bytes=56 * 1024 * 1024),
        cost_estimate=pl.CostEstimate(flops=int(us * 1.15e9), bytes_accessed=1 << 20, transcendentals=0),
    )(scalars, *args, *deps)


def whole(*shape):
    return pl.BlockSpec(shape, lambda i, s: (0,) * len(shape))


def part(*tail):
    return pl.BlockSpec((None,) + tail, lambda i, s: (i,) + (0,) * len(tail))


def near(*tail):
    return pl.BlockSpec((None,) + tail, lambda i, s: (jnp.maximum((i ^ s[0]) - 1, 0),) + (0,) * len(tail))


def rel(*tail):
    return pl.BlockSpec((None,) + tail, lambda i, s: (i ^ s[0],) + (0,) * len(tail))


def rel_out(*tail):
    return pl.BlockSpec((4, None) + tail, lambda i, s: (0, i ^ s[0]) + (0,) * len(tail))


def split_tail(v):
    value = v[16:24] + v[24:32]
    high = value.astype(BF16).astype(F32)
    return jnp.concatenate([v[0:16], high, value - high], 0).astype(BF16)


def sum_small_body(s, keep, got, *outs):
    for m in range(4):
        for k in range(keep.shape[1]):
            outs[m][k] = split_tail(total([keep[m, k], got[m, k]]))


def sum_small(place, keep, send, deps):
    shape = keep.shape
    return call(
        sum_small_body,
        (1,),
        [whole(*shape)] * 2,
        [whole(*shape[1:])] * 4,
        [(shape[1:], BF16)] * 4,
        [],
        place,
        [keep, swap(send, "dp", 1)],
        deps=deps,
    )


def sum_pair_body(s, keep, *refs):
    for m in range(4):
        refs[4 + m][...] = total([keep[m], refs[m][...]]).astype(BF16)


def sum_pair(place, keep, send, deps):
    zs, rows, cols = keep.shape[1:]
    return call(
        sum_pair_body,
        (zs,),
        [pl.BlockSpec((4, None, rows, cols), lambda i, s: (0, i, 0, 0))] + [part(rows, cols)] * 4,
        [part(rows, cols)] * 4,
        [((zs, rows, cols), BF16)] * 4,
        [],
        place,
        [keep] + [swap(send[m], "dp", 1) for m in range(4)],
        deps=deps,
    )


def plane_both_body(s, *refs):
    two, two_o, refs = refs[0], refs[-1], refs[1:-1]
    two_o[...] = two[...]
    zs = (len(refs) - 4) // 2
    small, outs = refs[:4], refs[4 + zs :]
    big = refs[4 : 4 + zs]
    rows = big[0].shape[0]
    for k in range(zs):
        outs[k][0:rows, :] = big[k][...]
        tail = split_tail(total([ref[k] for ref in small]))
        at = rows + TAIL_ROWS * k
        for out in outs:
            out[at : at + TAIL_ROWS, :] = tail


def plane_both(place, quarter, small, two, deps):
    zs = len(quarter)
    rows, cols = quarter[0].shape
    out = (rows + zs * TAIL_ROWS, cols)
    return call(
        plane_both_body,
        (1,),
        [whole(*two.shape)] + [whole(zs, TAIL_ROWS, cols)] * 4 + [whole(rows, cols)] * zs,
        [whole(*out)] * zs + [whole(*two.shape)],
        [(out, BF16)] * zs + [(two.shape, BF16)],
        [],
        place,
        [two, small[0]] + [swap(small[m], "dp", 2 * m) for m in range(1, 4)] + list(quarter),
        deps=deps,
    )


def line_both(place, quarter, deps):
    zs = len(quarter)
    rows, cols = quarter[0].shape
    first = rows - zs * TAIL_ROWS

    def body(s, *refs):
        ins, out = refs[:-1], refs[-1]
        out[0:first, :] = total([ref[0:first, :] for ref in ins]).astype(BF16)
        for b in range(zs):
            places = [first + TAIL_ROWS * (k ^ b) for k in range(zs)]
            parts = [ins[k][at : at + TAIL_ROWS, :] for k, at in enumerate(places)]
            at = first + TAIL_ROWS * b
            out[at : at + TAIL_ROWS, :] = split_tail(total(parts))

    def again(s, a, b, out):
        out[0:first, :] = total([a[0:first, :], b[0:first, :]]).astype(BF16)
        for at in range(first, rows, TAIL_ROWS):
            out[at : at + TAIL_ROWS, :] = split_tail(total([a[at : at + TAIL_ROWS, :], b[at : at + TAIL_ROWS, :]]))

    specs = [whole(rows, cols)]
    shape = [((rows, cols), BF16)]
    arrays = [quarter[0]] + [swap(q, "tensor", k) for k, q in enumerate(quarter) if k]
    mine = call(body, (1,), specs * zs, specs, shape, [], place, arrays, deps=deps)[0]
    bit = GROUP
    while bit < lax.axis_size("dp"):
        mine = call(again, (1,), specs * 2, specs, shape, [], place, [mine, swap(mine, "dp", bit)])[0]
        bit *= 2
    return mine


def plane_two_body(s, *refs):
    n = (len(refs) - 4) // 2
    ins, first, outs = refs[:4], refs[4 : 4 + n], refs[4 + n :]
    for k, out in enumerate(outs):
        out[0] = first[k][...]
        out[1] = total([ref[k] for ref in ins]).astype(out.dtype)


def plane_two(place, first, halves, deps):
    shape, dtype = halves[0].shape, halves[0].dtype
    return call(
        plane_two_body,
        (1,),
        [whole(*shape)] * 4 + [whole(*shape[1:])] * shape[0],
        [whole(2, *shape[1:])] * shape[0],
        [((2,) + shape[1:], dtype)] * shape[0],
        [],
        place,
        [halves[0]] + [swap(halves[m], "dp", 2 * m) for m in range(1, 4)] + list(first),
        deps=deps,
    )


def sum_pair_whole(place, keep, send, deps, us=4):
    zs, tail = keep.shape[1], keep.shape[2:]
    zeros = (0,) * len(tail)
    both = pl.BlockSpec((4, None) + tail, lambda i, s: (0, i) + zeros)

    def body(s, keep, got, *outs):
        for m in range(4):
            outs[m][...] = total([keep[m], got[m]]).astype(keep.dtype)

    return call(
        body,
        (zs,),
        [both] * 2,
        [part(*tail)] * 4,
        [((zs,) + tail, keep.dtype)] * 4,
        [],
        place,
        [keep, swap(send, "dp", 1)],
        us=us,
        deps=deps,
    )


def sum_plane_body(s, *refs):
    ins, outs = refs[:4], refs[4:]
    for k, out in enumerate(outs):
        out[...] = total([ref[k] for ref in ins]).astype(out.dtype)


def sum_plane(place, halves, deps):
    shape, dtype = halves[0].shape, halves[0].dtype
    return call(
        sum_plane_body,
        (1,),
        [whole(*shape)] * 4,
        [whole(*shape[1:])] * shape[0],
        [(shape[1:], dtype)] * shape[0],
        [],
        place,
        [halves[0]] + [swap(halves[m], "dp", 2 * m) for m in range(1, 4)],
        deps=deps,
    )


def sum_all_body(s, *refs):
    refs[-1][...] = total([ref[...] for ref in refs[:-1]]).astype(refs[-1].dtype)


def sum_all(place, arrays, deps):
    shape, dtype = arrays[0].shape, arrays[0].dtype
    specs = [whole(*shape)]
    return call(
        sum_all_body, (1,), specs * len(arrays), specs, [(shape, dtype)], [], place, arrays, deps=deps
    )[0]


def sum_line(place, quarter, deps):
    ds = lax.axis_size("dp")
    mine = sum_all(place, [quarter[0]] + [swap(q, "tensor", k) for k, q in enumerate(quarter) if k], deps)
    bit = GROUP
    while bit < ds:
        mine = sum_all(place, [mine, swap(mine, "dp", bit)], [])
        bit *= 2
    return mine


def assemble(s, own, pieces, out):
    i = pl.program_id(0)
    rows = pieces[0].shape[0]

    @pl.when(i == s[0])
    def _():
        out[...] = own[...]

    @pl.when(i != s[0])
    def _():
        for n in range(GROUP):
            place = pl.multiple_of((s[1] ^ n) * rows, rows)
            out[pl.ds(place, rows), :] = pieces[n][...]


def split_rows(s, full, keep, send):
    rows = full.shape[0] // GROUP
    for n in range(GROUP):
        place = pl.multiple_of((s[1] ^ n) * rows, rows)
        value = full[pl.ds(place, rows), :].astype(BF16)
        if n & 1 and len(send) == 1:
            send[0][n >> 1] = value
        elif n & 1:
            send[n >> 1][...] = value
        else:
            keep[n >> 1] = value


def iota(shape, dim):
    return lax.broadcasted_iota(jnp.int32, shape, dim)


def spread_sel(n, width, p):
    shape = (2 * LANES, width)
    return (iota(shape, 0) % LANES == iota(shape, 1) // p + n * SLOT).astype(BF16)


def gather_sel(n, width, p):
    shape = (width, LANES)
    return (iota(shape, 0) // p + n * SLOT == iota(shape, 1)).astype(BF16)


def head_lanes(heads, width, p):
    shape = (heads, width)
    return (iota(shape, 1) // p == iota(shape, 0)).astype(F32)


def flat_lanes(heads, width, first):
    shape = (heads, width)
    return (iota(shape, 1) == iota(shape, 0) + first).astype(F32)


def sigmoid(v):
    return 1.0 / (1.0 + jnp.exp(-v))


def softplus(v):
    return jnp.maximum(v, 0.0) + jnp.log1p(jnp.exp(-jnp.abs(v)))


def exact_sum(v, ones):
    a = v.astype(BF16)
    rest = v - a.astype(F32)
    b = rest.astype(BF16)
    c = (rest - b.astype(F32)).astype(BF16)
    return mm(a, ones) + mm(b, ones) + mm(c, ones)


def conv_rows(src, weight, bias, masks, count):
    taps = weight.shape[0]
    acc = bias + weight[taps - 1 : taps, :] * src[HALO : HALO + count, :]
    for j in range(1, taps):
        moved = src[HALO - j : HALO - j + count, :] * masks[:, j : j + 1]
        acc = acc + weight[taps - 1 - j : taps - j, :] * moved
    return acc


def conv_rows_back(pad, weight, masks_b, rows):
    taps = weight.shape[0]
    acc = weight[taps - 1 : taps, :] * pad[0:rows, :]
    for j in range(1, taps):
        acc = acc + weight[taps - 1 - j : taps - j, :] * (pad[j : j + rows, :] * masks_b[:, j : j + 1])
    return jnp.concatenate([acc[HALO:], acc[:HALO]], 0)


def slope(v):
    sig = sigmoid(v)
    return sig * (1.0 + v * (1.0 - sig))


def same_doc(dcol, drow, b, causal):
    shape = (CH, CH)
    column = dcol[HALO + b * CH : HALO + (b + 1) * CH, :]
    row = drow[:, b * CH : (b + 1) * CH]
    order = iota(shape, 0) >= iota(shape, 1) if causal else iota(shape, 0) <= iota(shape, 1)
    return (column == row) & order


def norm_body(s, hid, halo, gain, dcol, drow, w_bc, cw, cb,
              nx_o, inv_o, masks_o, masks_b_o, raw_o, bm_o, cm_o, bm_t_o, cm_t_o, gram_o, gram_t_o, scr):
    count = hid.shape[0]
    rows = HALO + count
    taps = cw.shape[0]
    n = bm_o.shape[1]
    ext = jnp.concatenate([hid[...], halo[...]], 0).astype(F32)
    inv = lax.rsqrt(jnp.mean(ext * ext, -1, keepdims=True) + epsilon)
    inv_o[...] = inv
    nx_o[...] = (ext * inv * gain[...]).astype(BF16)
    raw = mm(nx_o[...], w_bc[...])
    scr[0:HALO, :] = raw[count:]
    scr[HALO:, :] = raw[:count]
    raw_o[...] = scr[...]
    masks_o[...] = jnp.ones_like(masks_o)
    masks_b_o[...] = jnp.ones_like(masks_b_o)
    for j in range(1, taps):
        masks_o[:, j : j + 1] = (dcol[HALO - j : rows - j, :] == dcol[HALO:rows, :]).astype(F32)
        masks_b_o[:, j : j + 1] = (dcol[j : rows + j, :] == dcol[0:rows, :]).astype(F32)
    pre = conv_rows(scr, cw[...], cb[...], masks_o[...], count)
    states = pre * sigmoid(pre)
    flipped = states.T
    bm_o[...] = states[:, :n].astype(BF16)
    cm_o[...] = states[:, n:].astype(BF16)
    bm_t_o[...] = flipped[:n].astype(BF16)
    cm_t_o[...] = flipped[n:].astype(BF16)
    for b in range(count // CH):
        t = slice(b * CH, (b + 1) * CH)
        gram_o[b] = jnp.where(same_doc(dcol, drow, b, True), mm_nt(cm_o[t, :], bm_o[t, :]), 0.0)
        gram_t_o[b] = jnp.where(same_doc(dcol, drow, b, False), mm_nt(bm_o[t, :], cm_o[t, :]), 0.0)


def heads_body(s, pack, nx, dcol, drow, cum_o, pre_o, cols_o, parts_o, kap_o, dev_o, scr):
    heads, count = cum_o.shape
    width = pack.shape[1]
    p = width // heads
    flat = pack[FLAT : FLAT + 1, :]
    bias = jnp.sum(flat * flat_lanes(heads, width, 0), 1, keepdims=True)
    rate = -jnp.exp(jnp.sum(flat * flat_lanes(heads, width, heads), 1, keepdims=True))
    pre = bias
    for ch in range(nx.shape[1] // width):
        w = pack[W_DT + ch * heads : W_DT + (ch + 1) * heads, :].astype(BF16)
        pre = pre + mm_nt(w, nx[0:count, ch * width : (ch + 1) * width])
    pre_o[...] = pre
    step = softplus(pre)
    log_decay = step * rate
    ones = (iota((CH, CH), 0) <= iota((CH, CH), 1)).astype(BF16)
    spread = head_lanes(heads, width, p)
    scr[...] = jnp.zeros_like(scr)
    dev = None
    for b in range(count // CH):
        t = slice(b * CH, (b + 1) * CH)
        cum = exact_sum(log_decay[:, t], ones)
        cum_o[:, t] = cum
        end = cum[:, CH - 1 : CH]
        docs = drow[:, t]
        prev = dcol[HALO + b * CH - 1 : HALO + b * CH, :]
        last = dcol[HALO + (b + 1) * CH - 1 : HALO + (b + 1) * CH, :]
        fade = jnp.exp(end - cum) * (docs == last).astype(F32)
        for n, value in ((CUM, cum), (STEP, step[:, t]), (FADE, fade), (TAIL, fade * step[:, t]),
                         (HEAD, jnp.exp(cum) * (docs == prev).astype(F32))):
            scr[n * SLOT : n * SLOT + heads, t] = value
        kap = jnp.sum(jnp.exp(end) * (last == prev).astype(F32) * spread, 0, keepdims=True)
        kap_o[b : b + 1, :] = kap
        dev = kap if dev is None else dev * kap
    dev_o[...] = dev
    cols = scr[...].T
    cols_o[...] = cols
    high = cols.astype(BF16)
    parts_o[:, :LANES] = high
    parts_o[:, LANES:] = (cols - high.astype(F32)).astype(BF16)


def value_body(s, nx, own, *refs):
    pieces, (pack, masks, cols, b_t, kap, w_o, raw_o, xs_o, slope_o, e_o, dev_o, scr) = refs[:GROUP], refs[GROUP:]
    assemble(s, own, pieces, w_o)
    count, width = xs_o.shape
    taps = CONV_B
    raw = mm(nx[...], w_o[...])
    scr[0:HALO, :] = raw[count:]
    scr[HALO:, :] = raw[:count]
    raw_o[...] = scr[...].astype(BF16)
    pre = conv_rows(scr, pack[0:taps, :], pack[CONV_B : CONV_B + 1, :], masks[...], count)
    sig = sigmoid(pre)
    xs = pre * sig
    xs_o[...] = xs.astype(BF16)
    slope_o[...] = (sig * (1.0 + pre * (1.0 - sig))).astype(BF16)
    scaled = (xs * mm(cols[...], spread_sel(TAIL, width, HEAD_DIM))).astype(BF16)
    last = None
    for b in range(count // CH):
        fresh = mm(b_t[:, b * CH : (b + 1) * CH], scaled[b * CH : (b + 1) * CH])
        e_o[b] = fresh
        last = fresh if last is None else kap[b : b + 1, :] * last + fresh
    dev_o[...] = last.astype(BF16)


def gates_body(s, nx, cot, own, *refs):
    pieces, (wz_o, wo_o, z_o, d_o) = refs[:GROUP], refs[GROUP:]
    assemble(s, own.at[0], [ref.at[0] for ref in pieces], wz_o)
    assemble(s, own.at[1], [ref.at[1] for ref in pieces], wo_o)
    count, width = z_o.shape
    z_o[...] = mm(nx[0:count, :], wz_o[...]).astype(BF16)
    acc = None
    for ch in range(cot.shape[1] // width):
        c = slice(ch * width, (ch + 1) * width)
        term = mm_nt(cot[:, c], wo_o[c, :])
        acc = term if acc is None else acc + term
    d_o[...] = acc.astype(BF16)


def intra_body(s, xs, gram, cols, row, parts, pack, y_o):
    count, width = xs.shape
    heads = row.shape[0]
    p = width // heads
    x32 = xs[...].astype(F32)
    inputs = (x32 * mm(parts[...], spread_sel(STEP, width, p))).astype(BF16)
    left = iota((CH, 2 * p), 1) < p
    skip = pack[SKIP : SKIP + 1, :]
    for b in range(count // CH):
        t = slice(b * CH, (b + 1) * CH)
        a = gram[b]
        for pair in range(heads // 2):
            lanes = slice(2 * p * pair, 2 * p * (pair + 1))
            outs = []
            for h in (2 * pair, 2 * pair + 1):
                arg = jnp.minimum(cols[t, CUM * SLOT + h : CUM * SLOT + h + 1] - row[h : h + 1, t], 0.0)
                outs.append(mm((jnp.exp(arg) * a).astype(BF16), inputs[t, lanes]))
            y_o[t, lanes] = jnp.where(left, outs[0], outs[1]) + skip[:, lanes] * x32[t, lanes]


def carry_body(s, intra, cm, parts, e, kap, z_in, d_in, pack, *refs):
    parts_in, (y_o, state_o, sq_o, dot_o) = refs[:-4], refs[-4:]
    count, width = intra.shape
    scale = mm(parts[...], spread_sel(HEAD, width, HEAD_DIM))
    state = total([ref[...] for ref in parts_in])
    gain = pack[GAIN : GAIN + 1, :]

    @pl.when(pl.program_id(0) == 0)
    def _():
        sq_o[...] = jnp.zeros_like(sq_o)
        dot_o[...] = jnp.zeros_like(dot_o)

    for b in range(count // CH):
        t = slice(b * CH, (b + 1) * CH)
        low = state.astype(BF16)
        state_o[b] = low
        y = intra[t, :] + mm(cm[t, :], low) * scale[t]
        y_o[t, :] = y.astype(BF16)
        state = kap[b : b + 1, :] * state + e[b]
        z = z_in[t, :].astype(F32)
        gated = y * (z * sigmoid(z))
        sq = gated * gated
        dot = d_in[t, :].astype(F32) * gain * gated
        for lane in range(0, width, LANES):
            sq_o[t, :] += sq[:, lane : lane + LANES]
            dot_o[t, :] += dot[:, lane : lane + LANES]


def gate_back_body(s, y_in, z_in, d_in, pack, sq, dots, parts, c_t, kap, ng_o, dy_o, dz_o, gg_o, g_o, dev_o):
    count, width = y_in.shape
    channels = width * pl.num_programs(0)
    inv = lax.rsqrt(jnp.sum(sq[...], 1, keepdims=True) / channels + epsilon)
    coef = inv * inv * inv * (jnp.sum(dots[...], 1, keepdims=True) / channels)
    scale = mm(parts[...], spread_sel(HEAD, width, HEAD_DIM))
    gain = pack[GAIN : GAIN + 1, :]
    y = y_in[...].astype(F32)
    z = z_in[...].astype(F32)
    d_gate = d_in[...].astype(F32)
    sig = sigmoid(z)
    act = z * sig
    gated = y * act
    normed = gated * inv
    ng_o[...] = (normed * gain).astype(BF16)
    gg_o[...] = jnp.sum(d_gate * normed, 0, keepdims=True)
    d_gated = inv * (d_gate * gain) - gated * coef
    dy = d_gated * act
    dy_o[...] = dy.astype(BF16)
    dz_o[...] = (d_gated * y * (sig * (1.0 + z * (1.0 - sig)))).astype(BF16)
    scaled = (dy * scale).astype(BF16)
    back = None
    for b in reversed(range(count // CH)):
        t = slice(b * CH, (b + 1) * CH)
        fresh = mm(c_t[:, t], scaled[t])
        g_o[b] = fresh
        back = fresh if back is None else fresh + kap[b : b + 1, :] * back
    dev_o[...] = back.astype(BF16)


def out_body(s, ng, wo, cot, hid, keep, *refs):
    send, (out_o, acc, scr) = refs[:1], refs[1:]
    i = pl.program_id(0)
    width = ng.shape[1]

    @pl.when(i == 0)
    def _():
        acc[...] = hid[...].astype(F32)

    for ch in range(hid.shape[1] // width):
        c = slice(ch * width, (ch + 1) * width)
        acc[:, c] += mm(ng[...], wo[c, :])
        scr[c, :] = mm_tn(ng[...], cot[:, c])
    split_rows(s, scr, keep, send)

    @pl.when(i == pl.num_programs(0) - 1)
    def _():
        out_o[...] = acc[...].astype(BF16)


def gate_grad_body(s, dz, wz, nx_t, keep, *refs):
    send, (dn_o, scr) = refs[:1], refs[1:]

    @pl.when(pl.program_id(0) == 0)
    def _():
        dn_o[...] = jnp.zeros_like(dn_o)

    dn_o[...] += mm_nt(dz[...], wz[...])
    scr[...] = mm(nx_t[:, 0 : dz.shape[0]], dz[...])
    split_rows(s, scr, keep, send)


def intra_back_body(s, xs, dy, gram_t, cols, row, parts, du_o, col_o, row_o, dg_o):
    count, width = xs.shape
    heads = row.shape[0]
    p = width // heads
    inputs = (xs[...].astype(F32) * mm(parts[...], spread_sel(STEP, width, p))).astype(BF16)
    left = iota((CH, 2 * p), 1) < p
    zero = jnp.zeros((CH, 2 * p), BF16)
    col_o[...] = jnp.zeros_like(col_o)

    @pl.when(pl.program_id(0) == 0)
    def _():
        dg_o[...] = jnp.zeros_like(dg_o)

    for b in range(count // CH):
        t = slice(b * CH, (b + 1) * CH)
        a = gram_t[b]
        d_gram = None
        for pair in range(heads // 2):
            lanes = slice(2 * p * pair, 2 * p * (pair + 1))
            u_pair, dy_pair = inputs[t, lanes], dy[t, lanes]
            outs = []
            for n in (0, 1):
                h = 2 * pair + n
                u_one = jnp.where(left, u_pair, zero) if n == 0 else jnp.where(left, zero, u_pair)
                d_w = mm_nt(u_one, dy_pair)
                fade = jnp.exp(jnp.minimum(row[h : h + 1, t] - cols[t, CUM * SLOT + h : CUM * SLOT + h + 1], 0.0))
                w_t = fade * a
                moment = d_w * w_t
                d_gram = d_w * fade if d_gram is None else d_gram + d_w * fade
                lane = 3 * SLOT + h
                col_o[t, lane : lane + 1] = jnp.sum(moment, 1, keepdims=True)
                row_o[h : h + 1, t] = jnp.sum(moment, 0, keepdims=True)
                outs.append(mm(w_t.astype(BF16), dy_pair))
            du_o[t, lanes] = jnp.where(left, outs[0], outs[1])
        dg_o[b] += d_gram


def value_back_body(s, xs_in, dy_in, du_in, raw, slope_in, state, g, kap, parts, bm, cm, pack, masks, masks_b,
                    nx_t, w, *refs):
    parts_in, refs = refs[:-16], refs[-16:]
    keep, send, refs = refs[0], refs[1:5], refs[5:]
    dn_o, db_o, dc_o, hs_o, kg_o, sk_o, gc_o, scr, pad, full, dx = refs
    count, width = xs_in.shape
    p = HEAD_DIM
    taps = CONV_B
    cw = pack[0:taps, :]
    skip = pack[SKIP : SKIP + 1, :]

    @pl.when(pl.program_id(0) == 0)
    def _():
        dn_o[...] = jnp.zeros_like(dn_o)
        db_o[...] = jnp.zeros_like(db_o)
        dc_o[...] = jnp.zeros_like(dc_o)

    sums = [gather_sel(n, width, p) for n in range(3)]
    scr[...] = raw[...].astype(F32)
    pad[0:HALO, :] = jnp.zeros((HALO, width), F32)
    pad[HALO + count :, :] = jnp.zeros((HALO, width), F32)
    d_state = total([ref[...] for ref in parts_in])
    skip_sum = jnp.zeros((1, width), F32)
    for b in reversed(range(count // CH)):
        t = slice(b * CH, (b + 1) * CH)
        low = d_state.astype(BF16)
        xs = xs_in[t, :].astype(F32)
        dy = dy_in[t, :].astype(F32)
        scaled_x = (xs * mm(parts[t, :], spread_sel(TAIL, width, p))).astype(BF16)
        scaled_dy = (dy * mm(parts[t, :], spread_sel(HEAD, width, p))).astype(BF16)
        d_scaled = mm(bm[t, :], low)
        db_o[t, :] += mm_nt(scaled_x, low)
        dc_o[t, :] += mm_nt(scaled_dy, state[b])
        from_state = mm(cm[t, :], state[b]) * scaled_dy.astype(F32)
        to_state = d_scaled * scaled_x.astype(F32)
        kg_o[b : b + 1, :] = jnp.sum(d_state * state[b].astype(F32), 0, keepdims=True)
        du = du_in[t, :] + d_scaled * mm(parts[t, :], spread_sel(FADE, width, p))
        hs_o[t, :] = (
            mm(from_state.astype(BF16), sums[0])
            + mm(to_state.astype(BF16), sums[1])
            + mm((du * xs).astype(BF16), sums[2])
        )
        skip_sum = skip_sum + jnp.sum(dy * xs, 0, keepdims=True)
        d_xs = du * mm(parts[t, :], spread_sel(STEP, width, p)) + skip * dy
        pad[HALO + b * CH : HALO + (b + 1) * CH, :] = d_xs * slope_in[t, :].astype(F32)
        d_state = g[b] + kap[b : b + 1, :] * d_state
    sk_o[...] = skip_sum
    d_pre = pad[HALO : HALO + count, :]
    for j in range(taps):
        moved = scr[HALO - j : HALO - j + count, :] * d_pre
        if j:
            moved = moved * masks[:, j : j + 1]
        gc_o[taps - 1 - j : taps - j, :] = jnp.sum(moved, 0, keepdims=True)
    gc_o[taps : taps + 1, :] = jnp.sum(d_pre, 0, keepdims=True)
    dx[...] = conv_rows_back(pad, cw, masks_b, HALO + count).astype(BF16)
    dn_o[...] += mm_nt(dx[...], w[...])
    full[...] = mm(nx_t[...], dx[...])
    split_rows(s, full, keep, send)


def finish_body(s, pack, pre_dt, row_sums, col_sums, head_sums, kap, kap_sums, skip_sums, conv_sums, g_gain,
                d_gram_t, dcol, drow, bm, cm, db, dc, raw, cw, cb, masks, masks_b, nx, nx_t, w_bc, dn_x, dn_z,
                hid, halo, inv, keep, send, dn_o, gbc, blk, vec, ddt, wdt, scr, pad, small):
    i = pl.program_id(0)
    heads, count = pre_dt.shape
    rows = HALO + count
    width = pack.shape[1]
    dim = nx.shape[1]
    p = width // heads
    zs = pl.num_programs(0)
    n = bm.shape[1]
    taps = cw.shape[0]
    cols = 2 * n
    n_blocks = keep.shape[1]
    per_piece = gbc.shape[0] // (GROUP * n_blocks)
    half = cols * per_piece // width

    @pl.when(i == 0)
    def _():
        small[...] = jnp.zeros_like(small)
        ddt[...] = jnp.zeros_like(ddt)
        wdt[...] = jnp.zeros_like(wdt)
        vec[...] = jnp.zeros_like(vec)
        scr[...] = raw[...]
        pad[...] = jnp.zeros_like(pad)
        for b in range(count // CH):
            t = slice(b * CH, (b + 1) * CH)
            d_gram = jnp.where(same_doc(dcol, drow, b, False), d_gram_t[b], 0.0).astype(BF16)
            pad[HALO + b * CH : HALO + (b + 1) * CH, 0:n] = db[t, :] + mm(d_gram, cm[t, :])
            pad[HALO + b * CH : HALO + (b + 1) * CH, n:cols] = dc[t, :] + mm_tn(d_gram, bm[t, :])
        pre = conv_rows(scr, cw[...], cb[...], masks[...], count)
        d_pre = pad[HALO : HALO + count, :] * slope(pre)
        pad[HALO : HALO + count, :] = d_pre
        for j in range(taps):
            moved = scr[HALO - j : HALO - j + count, :] * d_pre
            if j:
                moved = moved * masks[:, j : j + 1]
            place = dim // cols + taps - 1 - j
            vec[place : place + 1, :] = jnp.sum(moved, 0, keepdims=True)
        place = dim // cols + taps
        vec[place : place + 1, :] = jnp.sum(d_pre, 0, keepdims=True)
        d_raw = conv_rows_back(pad, cw[...], masks_b[...], rows)
        high = d_raw.astype(BF16)
        low = (d_raw - high.astype(F32)).astype(BF16)
        gbc[...] = mm(nx_t[...], high) + mm(nx_t[...], low)
        dn_o[...] = dn_x[...] + mm_nt(high, w_bc[...]) + mm_nt(low, w_bc[...])
        dn_o[0:count, :] += dn_z[...]

    flat = pack[FLAT : FLAT + 1, :]
    rate = -jnp.exp(jnp.sum(flat * flat_lanes(heads, width, heads), 1, keepdims=True))
    pre = pre_dt[...]
    log_decay = softplus(pre) * rate
    sums = (head_sums[...] + col_sums[...]).T
    from_state = sums[0:heads]
    to_state = sums[SLOT : SLOT + heads]
    d_cum = row_sums[...] - sums[3 * SLOT : 3 * SLOT + heads] + from_state - to_state
    spread = head_lanes(heads, width, p)
    ones = (iota((CH, CH), 0) >= iota((CH, CH), 1)).astype(BF16)
    g_bias = jnp.zeros((heads, 1), F32)
    g_log = jnp.zeros((heads, 1), F32)
    place = pl.multiple_of(i * SLOT, SLOT)
    for b in range(count // CH):
        t = slice(b * CH, (b + 1) * CH)
        d_end = jnp.sum(to_state[:, t], 1, keepdims=True)
        d_end = d_end + jnp.sum(kap[b : b + 1, :] * kap_sums[b : b + 1, :] * spread, 1, keepdims=True)
        d_log = exact_sum(d_cum[:, t], ones) + d_end
        d_step = sums[2 * SLOT : 2 * SLOT + heads, t] + d_log * rate
        d_dt = d_step * sigmoid(pre[:, t])
        g_log = g_log + jnp.sum(d_log * log_decay[:, t], 1, keepdims=True)
        g_bias = g_bias + jnp.sum(d_dt, 1, keepdims=True)
        ddt[pl.ds(place, heads), t] = d_dt
    d_dt = ddt[pl.ds(place, heads), :].astype(BF16)

    def put(row, value):
        blk[row // 4, row % 4 : row % 4 + 1, :] = value

    blk[...] = jnp.zeros_like(blk)
    for r in range(taps + 1):
        put(r, conv_sums[r : r + 1, :])
    put(GAIN, g_gain[...])
    g_skip = jnp.sum(skip_sums[...] * spread, 1, keepdims=True)
    put(FLAT, jnp.sum(
        g_bias * flat_lanes(heads, width, 0)
        + g_log * flat_lanes(heads, width, heads)
        + g_skip * flat_lanes(heads, width, 2 * heads), 0, keepdims=True))
    for ch in range(dim // width):
        c = slice(ch * width, (ch + 1) * width)
        first = W_DT + ch * heads
        wdt[pl.ds(place, heads), c] = pack[first : first + heads, :]
        g_dt = mm(d_dt, nx[0:count, c])
        for h in range(heads):
            put(first + h, g_dt[h : h + 1, :])
    where = i ^ s[0]
    for m in range(GROUP):
        small[m, where, 16:20, :] = blk[s[1] ^ m, 0:4, :]

    @pl.when(i == zs - 1)
    def _():
        dn_o[0:count, :] += mm(ddt[...].T.astype(BF16), wdt[...].astype(BF16))
        weight_own = hid[...].astype(F32) * inv[0:count, :]
        weight_halo = halo[...].astype(F32) * inv[count:, :]
        g_norm = jnp.sum(dn_o[0:count, :] * weight_own, 0, keepdims=True)
        g_norm = g_norm + jnp.sum(dn_o[count:, :] * weight_halo, 0, keepdims=True)
        for c in range(dim // cols):
            vec[c : c + 1, :] = g_norm[:, c * cols : (c + 1) * cols]
        for m in range(GROUP):
            target = send if m & 1 else keep
            for k in range(n_blocks):
                at = (s[1] ^ m) * n_blocks + (k ^ s[0])
                for c in range(width // cols):
                    block = pl.multiple_of(at * per_piece + c * half, half)
                    small[m, k, 0:half, c * cols : (c + 1) * cols] = gbc[pl.ds(block, half), :]
                small[m, k, 20:21, 0:cols] = vec[pl.ds(at, 1), :]
                target[m >> 1, k] = split_tail(small[m, k])


def hidden_body(s, dn, later, hid, inv, gain, cot, out):
    count = hid.shape[0]

    def rows(t, d):
        scaled = d * gain[...]
        own = hid[t, :].astype(F32)
        r = inv[t, :]
        mean = jnp.mean(scaled * own, -1, keepdims=True)
        out[t, :] = cot[t, :].astype(F32) + r * scaled - own * (r * r * r * mean)

    rows(slice(0, count - HALO), dn[0 : count - HALO, :])
    rows(slice(count - HALO, count), dn[count - HALO : count, :] + later[...])


def hand_on_body(s, *refs):
    for k in range(3):
        refs[3 + k][...] = refs[k][...]


def scale_body(s, x, factor, out):
    out[...] = (x[...].astype(F32) * factor[...]).astype(BF16)


def join_two_body(s, *refs):
    pieces, (go, gz, scr) = refs[:2], refs[2:]
    rows, width = pieces[0].shape[2:]
    for n in range(GROUP):
        place = pl.multiple_of((s[1] ^ n) * rows, rows)
        scr[pl.ds(place, rows), :] = pieces[n & 1][n >> 1, 0].astype(F32)
        gz[pl.ds(place, rows), :] = pieces[n & 1][n >> 1, 1].astype(F32)
    for ch in range(go.shape[1] // width):
        c = slice(ch * width, (ch + 1) * width)
        go[:, c] = scr[c, :]


def join_all_body(s, *refs):
    pieces, (gx, gbc, blk, vec) = refs[:GROUP], refs[GROUP:]
    rows, width = gx.shape[0] // GROUP, gx.shape[1]
    cols = gbc.shape[1]
    zs = (pieces[0].shape[0] - rows) // TAIL_ROWS
    per_piece = gbc.shape[0] // (GROUP * zs)
    half = cols * per_piece // width
    for n in range(GROUP):
        a = s[1] ^ n
        gx[pl.ds(pl.multiple_of(a * rows, rows), rows), :] = pieces[n][0:rows, :].astype(F32)
        for k in range(zs):
            tail = pieces[n][rows + k * TAIL_ROWS : rows + (k + 1) * TAIL_ROWS, :].astype(F32)
            value = tail[16:24] + tail[24:32]
            at = a * zs + (k ^ s[0])
            if k == 0:
                blk[pl.ds(pl.multiple_of(a * SLOT, SLOT), SLOT), :] = value
            vec[pl.ds(pl.multiple_of(at * SLOT, SLOT), SLOT), :] = value
            for c in range(width // cols):
                block = pl.multiple_of(at * per_piece + c * half, half)
                gbc[pl.ds(block, half), :] = tail[0:half, c * cols : (c + 1) * cols]


def on_device(
    hidden,
    segment_ids,
    norm_gain,
    w_z,
    w_x,
    w_bc,
    w_dt,
    conv_x_w,
    conv_x_b,
    conv_bc_w,
    conv_bc_b,
    dt_bias,
    a_log,
    skip_d,
    gate_gain,
    w_out,
    cotangent,
):
    zs = lax.axis_size("tensor")
    z = lax.axis_index("tensor")
    piece_index = lax.axis_index("dp") & (GROUP - 1)
    place = jnp.stack([z, piece_index]).astype(jnp.int32)
    hid = hidden[0]
    cot = cotangent[0]
    count, dim = hid.shape
    taps, width = conv_x_w.shape
    heads = w_dt.shape[1]
    p = width // heads
    n = w_bc.shape[1] // 2
    blocks = count // CH
    rows = HALO + count
    chunks = dim // width
    wr = dim // GROUP

    halo = shift_up(hid[count - HALO :], "tensor", 1)
    flat = jnp.concatenate([dt_bias, a_log, skip_d])
    rows_f32 = jnp.concatenate(
        [
            conv_x_w,
            conv_x_b[None],
            gate_gain[None],
            jnp.repeat(skip_d, p)[None],
            jnp.pad(flat, (0, width - flat.shape[0]))[None],
        ],
        0,
    )
    high = lax.reduce_precision(rows_f32, 8, 7)
    by_chunk = w_dt.reshape(chunks, width, heads).transpose(0, 2, 1).reshape(chunks * heads, width)
    mine_x = lax.dynamic_slice_in_dim(w_x, piece_index * wr, wr, 0)
    message = jnp.concatenate([mine_x, high.astype(BF16), (rows_f32 - high).astype(BF16), by_chunk], 0)
    met = [swap(message, "tensor", k) for k in range(1, zs)]
    got_x = jnp.stack([m[:wr] for m in met], 0)
    tails = jnp.stack([message[wr:]] + [m[wr:] for m in met], 0).astype(F32)
    n_f32 = rows_f32.shape[0]
    pack = jnp.concatenate([tails[:, :n_f32] + tails[:, n_f32 : 2 * n_f32], tails[:, 2 * n_f32 :]], 1)
    out_chunks = w_out.reshape(width, chunks, width).transpose(1, 0, 2).reshape(dim, width)
    two = jnp.stack([w_z, out_chunks], 0)
    got_two = gather_blocks(lax.dynamic_slice_in_dim(two, piece_index * wr, wr, 1))
    x_pieces = spread_pieces(got_x)
    two_even = [got_two] + [swap(got_two, "dp", m) for m in (2, 4, 6)]

    docs = segment_ids[0].astype(F32)
    padded = jnp.concatenate([jnp.full((HALO,), -1.0, F32), docs])
    ext = lax.dynamic_slice_in_dim(padded, z * count, rows, 0)
    dcol = jnp.concatenate([ext, jnp.full((HALO,), -2.0, F32)])[:, None]
    drow = ext[None, HALO:]

    state_spec = part(blocks, n, width)
    dev_spec = part(n, width)
    wide = part(count, width)
    vec = part(1, width)
    kap_spec = part(blocks, width)
    gram_spec = whole(blocks, CH, CH)
    token_state = whole(count, n)
    state_token = whole(n, count)
    dcol_spec, drow_spec = whole(rows + HALO, 1), whole(1, count)
    mask_specs = [whole(count, SLOT), whole(rows, SLOT)]
    pack_spec = rel(pack.shape[1], width)
    parts_spec, cols_spec = part(count, 2 * LANES), part(count, LANES)
    row_spec = part(heads, count)
    bcw_specs = [whole(taps, 2 * n), whole(1, 2 * n)]
    big = (zs, count, width)
    states_shape = (zs, blocks, n, width)
    gain_row = norm_gain[None]
    cb_row = conv_bc_b[None]

    nx, inv, masks, masks_b, bc_raw, bm, cm, bm_t, cm_t, gram, gram_t = call(
        norm_body,
        (1,),
        [whole(count, dim), whole(HALO, dim), whole(1, dim), dcol_spec, drow_spec, whole(dim, 2 * n)] + bcw_specs,
        [whole(rows, dim), whole(rows, 1)]
        + mask_specs
        + [whole(rows, 2 * n), token_state, token_state, state_token, state_token, gram_spec, gram_spec],
        [
            ((rows, dim), BF16),
            ((rows, 1), F32),
            ((count, SLOT), F32),
            ((rows, SLOT), F32),
            ((rows, 2 * n), F32),
            ((count, n), BF16),
            ((count, n), BF16),
            ((n, count), BF16),
            ((n, count), BF16),
            ((blocks, CH, CH), F32),
            ((blocks, CH, CH), F32),
        ],
        [pltpu.VMEM((rows, 2 * n), F32)],
        place,
        [hid, halo, gain_row, dcol, drow, w_bc, conv_bc_w, cb_row],
        us=6,
        deps=[got_x],
    )
    nx_t = nx.T
    cum, pre_dt, cols, parts, kap, kap_dev = call(
        heads_body,
        (zs,),
        [pack_spec, whole(rows, dim), dcol_spec, drow_spec],
        [row_spec, row_spec, cols_spec, parts_spec, kap_spec, vec],
        [
            ((zs, heads, count), F32),
            ((zs, heads, count), F32),
            ((zs, count, LANES), F32),
            ((zs, count, 2 * LANES), BF16),
            ((zs, blocks, width), F32),
            ((zs, 1, width), F32),
        ],
        [pltpu.VMEM((LANES, count), F32)],
        place,
        [pack, nx, dcol, drow],
        us=4,
    )
    wx, raw, xs, slopes, e, dev = call(
        value_body,
        (zs,),
        [whole(rows, dim), whole(dim, width)]
        + [near(wr, width)] * GROUP
        + [pack_spec, mask_specs[0], parts_spec, state_token, kap_spec],
        [part(dim, width), part(rows, width), wide, wide, state_spec, dev_spec],
        [
            ((zs, dim, width), BF16),
            ((zs, rows, width), BF16),
            (big, BF16),
            (big, BF16),
            (states_shape, F32),
            ((zs, n, width), BF16),
        ],
        [pltpu.VMEM((rows, width), F32)],
        place,
        [nx, w_x, *x_pieces, pack, masks, parts, bm_t, kap],
        us=12,
    )

    steps = min(zs - 1, (DOC_MAX - 2) // count + 1)

    def pass_on(message, by, deps):
        got = []
        for k in range(steps):
            got.append(shift_up(message, "tensor", by))
            if k + 1 < steps:
                message = call(
                    scale_body, (1,), [whole(zs, n, width), whole(zs, 1, width)], [whole(zs, n, width)],
                    [((zs, n, width), BF16)], [], place, [got[-1], kap_dev], us=0.3, deps=deps,
                )[0]
        return got, message

    intra = call(
        intra_body,
        (zs,),
        [wide, gram_spec, cols_spec, row_spec, parts_spec, pack_spec],
        [wide],
        [(big, F32)],
        [],
        place,
        [xs, gram, cols, cum, parts, pack],
        us=8,
    )[0]
    carried, scaled = pass_on(dev, 1, [intra])
    copies = call(
        hand_on_body,
        (1,),
        [whole(*got_two.shape)] * 3,
        [whole(*got_two.shape)] * 3,
        [(got_two.shape, BF16)] * 3,
        [],
        place,
        two_even[1:],
        deps=[scaled],
    )
    two_pieces = []
    for even, sent in zip(two_even, [got_two] + list(copies)):
        two_pieces += [even, swap(sent, "dp", 1)]
    wz, wo, z_raw, d_gate = call(
        gates_body,
        (zs,),
        [whole(rows, dim), whole(count, dim), whole(2, dim, width)] + [near(2, wr, width)] * GROUP,
        [part(dim, width), part(dim, width), wide, wide],
        [((zs, dim, width), BF16), ((zs, dim, width), BF16), (big, BF16), (big, BF16)],
        [],
        place,
        [nx, cot, two, *two_pieces],
        us=14,
    )
    lanes = whole(count, LANES)
    y, state, squares, dots = call(
        carry_body,
        (zs,),
        [wide, token_state, parts_spec, state_spec, kap_spec, wide, wide, pack_spec] + [dev_spec] * steps,
        [wide, state_spec, lanes, lanes],
        [(big, BF16), (states_shape, BF16), ((count, LANES), F32), ((count, LANES), F32)],
        [],
        place,
        [intra, cm, parts, e, kap, z_raw, d_gate, pack, *carried],
        us=9,
    )
    ng, dy, dz, g_gain, g_state, g_dev = call(
        gate_back_body,
        (zs,),
        [wide, wide, wide, pack_spec, lanes, lanes, parts_spec, state_token, kap_spec],
        [wide, wide, wide, vec, state_spec, dev_spec],
        [(big, BF16)] * 3 + [((zs, 1, width), F32), (states_shape, F32), ((zs, n, width), BF16)],
        [],
        place,
        [y, z_raw, d_gate, pack, squares, dots, parts, cm_t, kap],
        us=10,
    )
    grad_specs = [rel_out(wr, width)] + [rel(wr, width)] * 4
    grad_shapes = [((4, zs, wr, width), BF16)] + [((zs, wr, width), BF16)] * 4
    keep_o, send_o, block_out = call(
        out_body,
        (zs,),
        [wide, part(dim, width), whole(count, dim), whole(count, dim)],
        [rel_out(wr, width)] * 2 + [whole(count, dim)],
        grad_shapes[:1] * 2 + [((count, dim), BF16)],
        [pltpu.VMEM((count, dim), F32), pltpu.VMEM((dim, width), F32)],
        place,
        [ng, wo, cot, hid],
        us=10,
    )
    keep_z, send_z, dn_z = call(
        gate_grad_body,
        (zs,),
        [wide, part(dim, width), whole(dim, rows)],
        [rel_out(wr, width)] * 2 + [whole(count, dim)],
        grad_shapes[:1] * 2 + [((count, dim), F32)],
        [pltpu.VMEM((dim, width), F32)],
        place,
        [dz, wz, nx_t],
        us=10,
        deps=[keep_o],
    )
    halves_o = sum_pair_whole(place, keep_o, send_o, [keep_z])
    from_later, scaled = pass_on(g_dev, -1, [halves_o[0]])
    du, col_sums, row_sums, d_gram_t = call(
        intra_back_body,
        (zs,),
        [wide, wide, gram_spec, cols_spec, row_spec, parts_spec],
        [wide, cols_spec, row_spec, gram_spec],
        [(big, F32), ((zs, count, LANES), F32), ((zs, heads, count), F32), ((blocks, CH, CH), F32)],
        [],
        place,
        [xs, dy, gram_t, cols, cum, parts],
        us=17,
        deps=[scaled],
    )
    halves_z = sum_pair_whole(place, keep_z, send_z, [du])
    quarter_o = sum_plane(place, halves_o, [halves_z[0]])
    keep_x, *send_x, dn_x, db, dc, head_sums, kap_sums, skip_sums, conv_sums = call(
        value_back_body,
        (zs,),
        [wide] * 3
        + [part(rows, width), wide, state_spec, state_spec, kap_spec, parts_spec, token_state, token_state]
        + [pack_spec]
        + mask_specs
        + [whole(dim, rows), part(dim, width)]
        + [dev_spec] * steps,
        grad_specs
        + [whole(rows, dim), token_state, token_state]
        + [cols_spec, kap_spec, vec, part(taps + 1, width)],
        grad_shapes
        + [
            ((rows, dim), F32),
            ((count, n), F32),
            ((count, n), F32),
            ((zs, count, LANES), F32),
            ((zs, blocks, width), F32),
            ((zs, 1, width), F32),
            ((zs, taps + 1, width), F32),
        ],
        [
            pltpu.VMEM((rows, width), F32),
            pltpu.VMEM((rows + HALO, width), F32),
            pltpu.VMEM((dim, width), F32),
            pltpu.VMEM((rows, width), BF16),
        ],
        place,
        [xs, dy, du, raw, slopes, state, g_state, kap, parts, bm, cm, pack, masks, masks_b, nx_t, wx, *from_later],
        us=28,
        deps=[quarter_o[0], halves_z[0]],
    )
    quarter_two = plane_two(place, quarter_o, halves_z, [dn_x])
    halves_x = sum_pair(place, keep_x, send_x, [quarter_two[0]])

    keep_s, send_s, dn = call(
        finish_body,
        (zs,),
        [pack_spec, row_spec, row_spec, cols_spec, cols_spec, kap_spec, kap_spec, vec, part(taps + 1, width), vec]
        + [gram_spec, dcol_spec, drow_spec] + [token_state] * 4 + [whole(rows, 2 * n)] + bcw_specs + mask_specs
        + [whole(rows, dim), whole(dim, rows), whole(dim, 2 * n), whole(rows, dim), whole(count, dim)]
        + [whole(count, dim), whole(HALO, dim), whole(rows, 1)],
        [whole(4, zs, TAIL_ROWS, width)] * 2 + [whole(rows, dim)],
        [((4, zs, TAIL_ROWS, width), BF16)] * 2 + [((rows, dim), F32)],
        [
            pltpu.VMEM((dim, 2 * n), F32),
            pltpu.VMEM((GROUP, SLOT, width), F32),
            pltpu.VMEM((GROUP * zs, 2 * n), F32),
            pltpu.VMEM((LANES, count), F32),
            pltpu.VMEM((LANES, dim), F32),
            pltpu.VMEM((rows, 2 * n), F32),
            pltpu.VMEM((rows + HALO, 2 * n), F32),
            pltpu.VMEM((GROUP, zs, TAIL_ROWS, width), F32),
        ],
        place,
        [pack, pre_dt, row_sums, col_sums, head_sums, kap, kap_sums, skip_sums, conv_sums, g_gain]
        + [d_gram_t, dcol, drow, bm, cm, db, dc, bc_raw, conv_bc_w, cb_row, masks, masks_b]
        + [nx, nx_t, w_bc, dn_x, dn_z, hid, halo, inv],
        us=13,
        deps=[halves_x[0]],
    )
    quarter_x = sum_plane(place, halves_x, [keep_s])
    halves_s = sum_small(place, keep_s, send_s, [quarter_x[0]])
    mine_two = sum_line(place, quarter_two, [halves_s[0]])
    *quarter, mine_two = plane_both(place, quarter_x, halves_s, mine_two, [])
    dn_later = shift_up(dn[count:], "tensor", -1)
    grad_hidden = call(
        hidden_body,
        (1,),
        [whole(rows, dim), whole(HALO, dim), whole(count, dim), whole(rows, 1), whole(1, dim), whole(count, dim)],
        [whole(count, dim)],
        [((count, dim), F32)],
        [],
        place,
        [dn, dn_later, hid, inv, gain_row, cot],
        us=5,
        deps=[quarter[0]],
    )[0]
    twos = jnp.stack([mine_two, swap(mine_two, "dp", 2)], 0)
    twos = jnp.concatenate([twos, swap(twos, "dp", 4)], 0)
    g_w_out, g_w_z = call(
        join_two_body,
        (1,),
        [whole(4, 2, wr, width)] * 2,
        [whole(width, dim), whole(dim, width)],
        [((width, dim), F32), ((dim, width), F32)],
        [pltpu.VMEM((dim, width), F32)],
        place,
        [twos, swap(twos, "dp", 1)],
    )
    mine = line_both(place, quarter, [grad_hidden])
    all_out = spread_pieces(mine)
    g_w_x, g_w_bc, blk, vec_rows = call(
        join_all_body,
        (1,),
        [whole(*mine.shape)] * GROUP,
        [whole(dim, width), whole(dim, 2 * n), whole(GROUP * SLOT, width), whole(GROUP * zs * SLOT, width)],
        [((dim, width), F32), ((dim, 2 * n), F32), ((GROUP * SLOT, width), F32), ((GROUP * zs * SLOT, width), F32)],
        [],
        place,
        all_out,
    )
    blocked = blk.reshape(GROUP, SLOT, width)[:, :4].reshape(4 * GROUP, width)
    vecs = vec_rows.reshape(GROUP * zs, SLOT, width)[:, 4, : 2 * n]
    flat = blocked[FLAT]
    g_w_dt = blocked[W_DT : W_DT + chunks * heads].reshape(chunks, heads, width).transpose(0, 2, 1).reshape(dim, heads)
    lead = dim // (2 * n)
    return (
        block_out[None],
        grad_hidden[None],
        vecs[:lead].reshape(dim),
        g_w_z,
        g_w_x,
        g_w_bc,
        g_w_dt,
        blocked[:taps],
        blocked[taps],
        vecs[lead : lead + taps],
        vecs[lead + taps],
        flat[:heads],
        flat[heads : 2 * heads],
        flat[2 * heads : 3 * heads],
        blocked[GAIN],
        g_w_out,
    )


def solution(mesh):
    placed = (
        P("dp", "tensor", None),
        P("dp", None),
        P(),
        P(None, "tensor"),
        P(None, "tensor"),
        P(),
        P(None, "tensor"),
        P(None, "tensor"),
        P("tensor"),
        P(),
        P(),
        P("tensor"),
        P("tensor"),
        P("tensor"),
        P("tensor"),
        P("tensor", None),
        P("dp", "tensor", None),
    )
    return jax.shard_map(
        on_device,
        mesh=mesh,
        in_specs=placed,
        out_specs=(
            P("dp", "tensor", None),
            P("dp", "tensor", None),
            P(),
            P(None, "tensor"),
            P(None, "tensor"),
            P(),
            P(None, "tensor"),
            P(None, "tensor"),
            P("tensor"),
            P(),
            P(),
            P("tensor"),
            P("tensor"),
            P("tensor"),
            P("tensor"),
            P("tensor", None),
        ),
        check_vma=False,
    )
```
